128 devices in a mesh: band: 8 (over x, y_lo), row: 16 (over z, y_hi, core).
Axes of the slice: x: 4, y: 4 (y_hi: 2, y_lo: 2; y = y_hi * 2 + y_lo), z: 4, core: 2. Of those that a mesh axis runs over, the one named last changes fastest.
Arguments:
- phase: float32 [4096, 4096], P('row'), may hold values from -3.140625 to 3.140625
- aperture: int32 [4096, 4096], P('row'), may hold values 0 or 1
- defocus_index: int32 [16], P('band'), may hold values from 0 to 3
- intensity: float32 [16, 512, 512], P('band', 'row'), may hold values from 0.1 to 3
Outputs:
- gradient: float32 [4096, 4096], P('row', 'band')
The draws below stay inside these ranges and needn't reach their ends.
All inputs are finite; a program needn't handle non-finite values. No bound on the sum of `aperture` on one device may be relied on, other than what follows from the above.
Results may differ from the reference program's by a relative error of at most 0.0032.
Values may be sent and summed in bfloat16 or wider, within the bound.
No kernel may reach another device: no remote copies, remote signals or barrier semaphores. Data moves between devices by JAX's collectives and lax.ppermute only.
A program may use at most 128 MiB of HBM per device.

```python
import math
import jax
import jax.numpy as jnp
from jax import lax

P_SIZE = 4096
M = 512
WAVES = 16


def touch_ends(values, stream_key, low, largest):
    longest = values.shape.index(max(values.shape))
    spots = []
    for shift in (0, 1):
        where = [jax.random.randint(jax.random.fold_in(stream_key, axis), (), 0, length) for axis, length in enumerate(values.shape)]
        where[longest] = (where[longest] + shift) % values.shape[longest]
        spots.append(tuple(where))
    return values.at[spots[0]].set(low).at[spots[1]].set(largest)


def levels(own_key, extent, split, smallest, top_value):
    def one(dim, parts):
        draws = jax.random.uniform(jax.random.fold_in(jax.random.fold_in(own_key, 6), dim), (parts,), jnp.float32, smallest / len(split), top_value / len(split))
        return jnp.repeat(jnp.exp(draws), extent[dim] // parts).reshape((-1,) + (1,) * (len(extent) - dim - 1))

    level = one(*split[0])
    for cut in split[1:]:
        level = level * one(*cut)
    return level


def setup_inputs(seed: int = 0) -> dict:
    streams_of = jax.random.split(jax.random.key(seed), 5)
    phase = jnp.clip(jax.random.uniform(streams_of[0], (P_SIZE, P_SIZE), jnp.float32, -3.140625, 3.140625), -3.140625, 3.140625)
    aperture = touch_ends((jax.random.randint(streams_of[1], (P_SIZE, P_SIZE), 0, 4) < 3).astype(jnp.int32), jax.random.fold_in(streams_of[1], 1), 0, 1)
    defocus_index = touch_ends(jax.random.randint(streams_of[2], (WAVES,), 0, 4), jax.random.fold_in(streams_of[2], 1), 0, 3).astype(jnp.int32)
    intensity = jnp.clip(jnp.exp(math.log(3.0) - 3.4011974 * jax.random.uniform(streams_of[3], (WAVES, M, M), jnp.float32) ** levels(streams_of[3], (WAVES, M, M), ((0, 8), (1, 16)), -0.2, 0.2)), 0.1, 3.0)
    return dict(phase=phase, aperture=aperture, defocus_index=defocus_index, intensity=intensity)


defocus_strength = math.pi

def focal_table(wave_index, waves, focal_width, pupil_width):
    scale_ratio = 1.0 / (1.0 + wave_index.astype(jnp.float32) / waves)
    column = 2 * lax.broadcasted_iota(jnp.int32, (focal_width, pupil_width), 1) - pupil_width + 1
    offset = 2 * lax.broadcasted_iota(jnp.int32, (focal_width, pupil_width), 0) - focal_width
    phase_angle = (column * offset).astype(jnp.float32) * (scale_ratio * (math.pi / (4.0 * pupil_width)))
    normalizer = 1.0 / math.sqrt(pupil_width)
    return jnp.stack([jnp.cos(phase_angle) * normalizer, -jnp.sin(phase_angle) * normalizer]).astype(jnp.bfloat16)

def pupil_field(phase, aperture, defocus_level, first_row, pupil_width):
    row_pos = (2 * (first_row + lax.broadcasted_iota(jnp.int32, phase.shape, 0)) - pupil_width + 1).astype(jnp.float32)
    col_pos = (2 * lax.broadcasted_iota(jnp.int32, phase.shape, 1) - pupil_width + 1).astype(jnp.float32)
    radius = (row_pos * row_pos + col_pos * col_pos) / float(pupil_width * pupil_width)
    shifted = phase + defocus_level.astype(jnp.float32) * defocus_strength * radius
    amplitude = aperture.astype(jnp.float32)
    return (amplitude * jnp.cos(shifted), amplitude * jnp.sin(shifted))

def mat(left, right):
    return jnp.dot(left, right, preferred_element_type=jnp.float32)

def reference(phase, aperture, defocus_index, intensity):

    def one_wave(wave_index, running):
        wave_index = wave_index.astype(jnp.int32)
        table = focal_table(wave_index, WAVES, M, P_SIZE)
        table_re = table[0]
        table_im = table[1]
        defocus_level = lax.dynamic_index_in_dim(defocus_index, wave_index, 0, keepdims=False)
        field_re, field_im = pupil_field(phase, aperture, defocus_level, jnp.int32(0), P_SIZE)
        pupil_re = field_re.astype(jnp.bfloat16)
        pupil_im = field_im.astype(jnp.bfloat16)
        product_re = (mat(pupil_re, table_re.T) - mat(pupil_im, table_im.T)).astype(jnp.bfloat16)
        product_im = (mat(pupil_re, table_im.T) + mat(pupil_im, table_re.T)).astype(jnp.bfloat16)
        focal_re = mat(product_re.T, table_re.T) - mat(product_im.T, table_im.T)
        focal_im = mat(product_re.T, table_im.T) + mat(product_im.T, table_re.T)
        observed = lax.dynamic_index_in_dim(intensity, wave_index, 0, keepdims=False)
        misfit = focal_re * focal_re + focal_im * focal_im - observed
        weighted_re = (misfit * focal_re).astype(jnp.bfloat16)
        weighted_im = (misfit * focal_im).astype(jnp.bfloat16)
        back_re = (mat(table_re.T, weighted_re.T) + mat(table_im.T, weighted_im.T)).astype(jnp.bfloat16)
        back_im = (mat(table_re.T, weighted_im.T) - mat(table_im.T, weighted_re.T)).astype(jnp.bfloat16)
        spread_re = mat(back_re, table_re) + mat(back_im, table_im)
        spread_im = mat(back_im, table_re) - mat(back_re, table_im)
        return running + (spread_im * field_re - spread_re * field_im)
    return lax.fori_loop(jnp.int32(0), jnp.int32(WAVES), one_wave, jnp.zeros((P_SIZE, P_SIZE), jnp.float32))
```

```python
import math

import jax
import jax.numpy as jnp
from jax import lax
from jax.experimental import pallas as pl
from jax.experimental.pallas import tpu as pltpu
from jax.sharding import PartitionSpec as P

F32 = jnp.float32
BF16 = jnp.bfloat16
N = 4096
M = 512
HALF = N // 2
K = M // 2
ROWS = 256
BLK = 256
STEPS = HALF // BLK
WL = 2
GRP = 32
NORM = 1.0 / math.sqrt(N)

SIN_C = (9.99999246e-01, -1.66656827e-01, 8.31325871e-03, -1.85243573e-04)
COS_C = (9.99999953e-01, -4.99999053e-01, 4.16635847e-02, -1.38537043e-03, 2.31539316e-05)
SIN_T = (6.28318492, -41.34159016, 81.5999729, -76.61480386, 41.34439753, -12.47366849)
COS_T = (0.99999999, -19.73920453, 64.93911898, -85.45016555, 60.16783172, -25.96831326, 6.52961036)


def poly(coefs, y):
    acc = coefs[-1]
    for c in coefs[-2::-1]:
        acc = acc * y + c
    return acc


def turn(t):
    t = t - jnp.floor(t + 0.5)
    y = t * t
    return poly(COS_T, y), t * poly(SIN_T, y)


def unit(phi):
    y = phi * phi
    r2 = math.sqrt(2.0)
    c = poly([r2 * v / 4.0**n for n, v in enumerate(COS_C)], y)
    s = phi * poly([0.5 * r2 * v / 4.0**n for n, v in enumerate(SIN_C)], y)
    return c, s


def field(phi, amp):
    c, s = unit(phi)
    a_s = amp * s
    return amp - s * a_s, a_s * c


def lane_rev(x):
    rows, lanes = x.shape
    idx = 127 - lax.broadcasted_iota(jnp.int32, (rows, 128), 1)
    parts = [
        jnp.take_along_axis(x[:, s : s + 128], idx, axis=1, mode="promise_in_bounds")
        for s in range(lanes - 128, -1, -128)
    ]
    return jnp.concatenate(parts, axis=1) if len(parts) > 1 else parts[0]


def nt(a, b):
    return lax.dot_general(a, b, (((1,), (1,)), ((), ())), preferred_element_type=F32)


def nn(a, b):
    return lax.dot_general(a, b, (((1,), (0,)), ((), ())), preferred_element_type=F32)


def span(meta, w):
    return (1024 * (16 + meta[1] + w)).astype(F32)


def angle(n, m):
    inv = 1.0 / m
    q = jnp.floor(n * inv + 0.5)
    return turn((n - q * m) * inv)


def chirp_cols(meta, w, first, lanes):
    x = (2 * (first + lax.broadcasted_iota(jnp.int32, (1, lanes), 1)) + 1).astype(F32)
    return turn(x * x * (meta[2 + w].astype(F32) * (0.5 / (N * N))))


def chirp_rows(meta, w, row_pos):
    x = (2 * row_pos - (N - 1)).astype(F32)
    return turn(x * x * (meta[2 + w].astype(F32) * (0.5 / (N * N))))


def flip_matrix(flip):
    r = lax.broadcasted_iota(jnp.int32, (ROWS, ROWS), 0)
    c = lax.broadcasted_iota(jnp.int32, (ROWS, ROWS), 1)
    return jnp.where(jnp.where(flip, ROWS - 1 - c, c) == r, 1.0, 0.0).astype(BF16)


def forward_kernel(meta, ph_r, ph_l, ap_r, ap_l, tab, fld, out, z, rot, e_s, o_s, xacc, yacc, tmp):
    i = pl.program_id(0)

    @pl.when(i == 0)
    def _():
        xacc[...] = jnp.zeros_like(xacc)
        yacc[...] = jnp.zeros_like(yacc)
        for w in range(WL):
            m = span(meta, w)

            def init(t, _):
                r0 = pl.multiple_of(t * 32, 32)
                k = lax.broadcasted_iota(jnp.int32, (32, BLK), 0) + (r0 + 1)
                j = 2 * lax.broadcasted_iota(jnp.int32, (32, BLK), 1) + 1
                c, s = angle((k * j).astype(F32), m)
                z[w, 0, pl.ds(r0, 32), :] = c * NORM
                z[w, 1, pl.ds(r0, 32), :] = s * NORM
                k = lax.broadcasted_iota(jnp.int32, (32, 128), 0) + (r0 + 1)
                c, s = angle((k * (2 * BLK)).astype(F32), m)
                rot[w, 0, pl.ds(r0, 32), :] = c
                rot[w, 1, pl.ds(r0, 32), :] = s
                return 0

            lax.fori_loop(0, 8, init, 0)

    @pl.when(i > 0)
    def _():
        for w in range(WL):

            def step(t, _):
                r0 = pl.multiple_of(t * 32, 32)
                rc, rs = rot[w, 0, pl.ds(r0, 32), :], rot[w, 1, pl.ds(r0, 32), :]
                for h in (0, 128):
                    zc = z[w, 0, pl.ds(r0, 32), h : h + 128]
                    zs = z[w, 1, pl.ds(r0, 32), h : h + 128]
                    z[w, 0, pl.ds(r0, 32), h : h + 128] = zc * rc - zs * rs
                    z[w, 1, pl.ds(r0, 32), h : h + 128] = zc * rs + zs * rc
                return 0

            lax.fori_loop(0, 8, step, 0)

    dx = [chirp_cols(meta, w, i * BLK, BLK) for w in range(WL)]

    def rows(t, _):
        r0 = pl.multiple_of(t * 32, 32)
        sl = pl.ds(r0, 32)
        fr_c, fr_s = field(ph_r[sl, :], ap_r[sl, :].astype(F32))
        fl_c, fl_s = field(lane_rev(ph_l[sl, :]), lane_rev(ap_l[sl, :].astype(F32)))
        fld[0, sl, :] = fr_c
        fld[1, sl, :] = fr_s
        fld[2, sl, :] = fl_c
        fld[3, sl, :] = fl_s
        ec, es = fr_c + fl_c, fr_s + fl_s
        oc, os = fr_c - fl_c, fr_s - fl_s
        for w in range(WL):
            dc, ds = dx[w]
            e_s[w, 0, sl, :] = (ec * dc - es * ds).astype(BF16)
            e_s[w, 1, sl, :] = (ec * ds + es * dc).astype(BF16)
            o_s[w, 0, sl, :] = (oc * dc - os * ds).astype(BF16)
            o_s[w, 1, sl, :] = (oc * ds + os * dc).astype(BF16)
        return 0

    lax.fori_loop(0, ROWS // 32, rows, 0)
    ones = jnp.full((16, BLK), NORM, BF16)
    for w in range(WL):
        c = z[w, 0].astype(BF16)
        s = z[w, 1].astype(BF16)
        tab[w, 0] = c
        tab[w, 1] = s
        c = jnp.concatenate([c, ones], axis=0)
        for part in range(2):
            xacc[w, part] += nt(c, e_s[w, part])
            yacc[w, part] += nt(s, o_s[w, part])

    @pl.when(i == STEPS - 1)
    def _():
        row0 = meta[0] * ROWS
        j = flip_matrix(meta[0] < 8)
        pos = row0 + lax.broadcasted_iota(jnp.int32, (1, ROWS), 1)
        for w in range(WL):
            dc, ds = chirp_rows(meta, w, pos)
            xr, xi = xacc[w, 0], xacc[w, 1]
            yr, yi = yacc[w, 0], yacc[w, 1]
            xr, xi = xr * dc - xi * ds, xr * ds + xi * dc
            yr, yi = yr * dc - yi * ds, yr * ds + yi * dc
            x0 = (xr[K : K + 1], xi[K : K + 1])
            xr, xi = xr[:K], xi[:K]
            plus = (xr + yi, xi - yr)
            minus = (xr - yi, xi + yr)
            for part in range(2):
                tmp[pl.ds(8, K), :] = plus[part]
                tmp[pl.ds(7, 1), :] = x0[part]
                p = nn(tmp[pl.ds(7, K), :].astype(BF16), j).astype(BF16)
                m = nn(minus[part].astype(BF16), j).astype(BF16)
                at = (w * 2 + part) * GRP
                for g in range(8):
                    out[8 + g, at : at + GRP, :] = p[g * GRP : (g + 1) * GRP]
                    out[7 - g, at : at + GRP, :] = m[g * GRP : (g + 1) * GRP]


def focal_kernel(x, tab, obs, out):
    last = lax.broadcasted_iota(jnp.int32, (GRP, K), 1) == K - 1
    for w in range(WL):
        at = w * 2 * GRP
        acc_c = jnp.zeros((2 * GRP, K), F32)
        acc_s = jnp.zeros((2 * GRP, K), F32)
        centre = jnp.zeros((2 * GRP, BLK), F32)
        for i in range(STEPS):
            r = x[8 + i, at : at + 2 * GRP, :].astype(F32)
            l = x[7 - i, at : at + 2 * GRP, :].astype(F32)
            e = r + l
            centre = centre + e
            cols = slice(i * BLK, (i + 1) * BLK)
            acc_c = acc_c + nt(e.astype(BF16), tab[w, 0, :, cols])
            acc_s = acc_s + nt((r - l).astype(BF16), tab[w, 1, :, cols])
        centre = jnp.sum(centre, axis=1, keepdims=True) * NORM
        cr, ci = acc_c[:GRP], acc_c[GRP:]
        sr, si = acc_s[:GRP], acc_s[GRP:]
        weighted = []
        for side, (fr, fi) in enumerate(
            (
                (jnp.where(last, centre[:GRP], cr + si), jnp.where(last, centre[GRP:], ci - sr)),
                (cr - si, ci + sr),
            )
        ):
            misfit = fr * fr + fi * fi - obs[w, :, side * K : (side + 1) * K]
            weighted.append(
                [(misfit * fr).astype(BF16).astype(F32), (misfit * fi).astype(BF16).astype(F32)]
            )
        (pr, pi), (mr, mi) = weighted
        centre = jnp.concatenate([pr[:, K - 1 :], pi[:, K - 1 :]], axis=0) * NORM
        p = jnp.concatenate([jnp.where(last, 0.0, pr), jnp.where(last, 0.0, pi)], axis=0)
        m = jnp.concatenate([mr, mi], axis=0)
        s = (p + m).astype(BF16)
        d = (p - m).astype(BF16)
        for i in range(STEPS):
            cols = slice(i * BLK, (i + 1) * BLK)
            bc = nn(s, tab[w, 0, :, cols]) + centre
            bs = nn(d, tab[w, 1, :, cols])
            bcr, bci, bsr, bsi = bc[:GRP], bc[GRP:], bs[:GRP], bs[GRP:]
            out[8 + i, at : at + GRP, :] = (bcr - bsi).astype(BF16)
            out[8 + i, at + GRP : at + 2 * GRP, :] = (bci + bsr).astype(BF16)
            out[7 - i, at : at + GRP, :] = (bcr + bsi).astype(BF16)
            out[7 - i, at + GRP : at + 2 * GRP, :] = (bci - bsr).astype(BF16)


def gradient_kernel(meta, x, tab, fld, out, lhs, mid, sp, tmp):
    i = pl.program_id(0)

    @pl.when(i == 0)
    def _():
        flip = meta[0] < 8
        j = flip_matrix(flip)
        lane = lax.broadcasted_iota(jnp.int32, (1, ROWS), 1)
        pos = meta[0] * ROWS + jnp.where(flip, ROWS - 1 - lane, lane)
        for w in range(WL):
            dc, ds = chirp_rows(meta, w, pos)
            p, m, b0 = [], [], []
            for part in range(2):
                at = (w * 2 + part) * GRP
                for g in range(8):
                    tmp[g * GRP : (g + 1) * GRP, :] = x[8 + g, at : at + GRP, :].astype(F32)
                tmp[K : K + 8, :] = jnp.zeros((8, ROWS), F32)
                b0.append(tmp[0:1, :])
                p.append(tmp[pl.ds(1, K), :])
                m.append(
                    jnp.concatenate([x[7 - g, at : at + GRP, :] for g in range(8)], axis=0).astype(F32)
                )
            for n, (re, im) in enumerate(
                ((p[0] + m[0], p[1] + m[1]), (p[0] - m[0], p[1] - m[1]))
            ):
                lhs[w, 2 * n] = nt(j, (re * dc + im * ds).astype(BF16)).astype(BF16)
                lhs[w, 2 * n + 1] = nt(j, (im * dc - re * ds).astype(BF16)).astype(BF16)
            for part, v in enumerate((b0[0] * dc + b0[1] * ds, b0[1] * dc - b0[0] * ds)):
                v = jnp.broadcast_to((v * NORM).astype(BF16), (128, ROWS))
                mid[w, part] = nt(j, v)

    for w in range(WL):
        c = tab[w, 0]
        s = tab[w, 1]
        for part in range(2):
            sp[w, part] = nn(lhs[w, part], c)
            sp[w, 2 + part] = nn(lhs[w, 2 + part], s)
    dx = [chirp_cols(meta, w, i * BLK, BLK) for w in range(WL)]
    right = 4 + i // 2, pl.multiple_of((i % 2) * BLK, BLK)
    left = 3 - i // 2, pl.multiple_of((1 - i % 2) * BLK, BLK)

    def rows(t, _):
        r0 = pl.multiple_of(t * 32, 32)
        sl = pl.ds(r0, 32)
        tot = [0.0, 0.0, 0.0, 0.0]
        for w in range(WL):
            dc, ds = dx[w]
            m = [jnp.concatenate([mid[w, part, sl, :]] * 2, axis=1) for part in range(2)]
            cr, ci = sp[w, 0, sl, :] + m[0], sp[w, 1, sl, :] + m[1]
            sr, si = sp[w, 2, sl, :], sp[w, 3, sl, :]
            tot[0] += cr * dc + ci * ds
            tot[1] += ci * dc - cr * ds
            tot[2] += sr * dc + si * ds
            tot[3] += si * dc - sr * ds
        cr, ci, sr, si = tot
        g_r = (ci + sr) * fld[0, sl, :] - (cr - si) * fld[1, sl, :]
        g_l = (ci - sr) * fld[2, sl, :] - (cr + si) * fld[3, sl, :]
        out[right[0], sl, pl.ds(right[1], BLK)] = g_r.astype(BF16)
        out[left[0], sl, pl.ds(left[1], BLK)] = lane_rev(g_l).astype(BF16)
        return 0

    lax.fori_loop(0, ROWS // 32, rows, 0)


def run_forward(meta, phase, aperture):
    smem = pl.BlockSpec(memory_space=pltpu.SMEM)
    right = pl.BlockSpec((ROWS, BLK), lambda i: (0, STEPS + i))
    left = pl.BlockSpec((ROWS, BLK), lambda i: (0, STEPS - 1 - i))
    return pl.pallas_call(
        forward_kernel,
        grid=(STEPS,),
        out_shape=(
            jax.ShapeDtypeStruct((WL, 2, K, HALF), BF16),
            jax.ShapeDtypeStruct((4, ROWS, HALF), F32),
            jax.ShapeDtypeStruct((16, WL * 2 * GRP, ROWS), BF16),
        ),
        in_specs=[smem, right, left, right, left],
        out_specs=(
            pl.BlockSpec((WL, 2, K, BLK), lambda i: (0, 0, 0, i)),
            pl.BlockSpec((4, ROWS, BLK), lambda i: (0, 0, i)),
            pl.BlockSpec((16, WL * 2 * GRP, ROWS), lambda i: (0, 0, 0)),
        ),
        scratch_shapes=[
            pltpu.VMEM((WL, 2, K, BLK), F32),
            pltpu.VMEM((WL, 2, K, 128), F32),
            pltpu.VMEM((WL, 2, ROWS, BLK), BF16),
            pltpu.VMEM((WL, 2, ROWS, BLK), BF16),
            pltpu.VMEM((WL, 2, K + 16, ROWS), F32),
            pltpu.VMEM((WL, 2, K, ROWS), F32),
            pltpu.VMEM((K + 16, ROWS), F32),
        ],
        compiler_params=pltpu.CompilerParams(vmem_limit_bytes=40 * 2**20),
        name="forward",
    )(meta, phase, phase, aperture, aperture)


def run_focal(x, tab, obs):
    return pl.pallas_call(
        focal_kernel,
        out_shape=jax.ShapeDtypeStruct((16, WL * 2 * GRP, ROWS), BF16),
        in_specs=[pl.BlockSpec(memory_space=pltpu.VMEM)] * 3,
        out_specs=pl.BlockSpec(memory_space=pltpu.VMEM),
        compiler_params=pltpu.CompilerParams(vmem_limit_bytes=32 * 2**20),
        name="focal",
    )(x, tab, obs)


def run_gradient(meta, x, tab, fld):
    return pl.pallas_call(
        gradient_kernel,
        grid=(STEPS,),
        out_shape=jax.ShapeDtypeStruct((8, ROWS, M), BF16),
        in_specs=[
            pl.BlockSpec(memory_space=pltpu.SMEM),
            pl.BlockSpec((16, WL * 2 * GRP, ROWS), lambda i: (0, 0, 0)),
            pl.BlockSpec((WL, 2, K, BLK), lambda i: (0, 0, 0, i)),
            pl.BlockSpec((4, ROWS, BLK), lambda i: (0, 0, i)),
        ],
        out_specs=pl.BlockSpec((8, ROWS, M), lambda i: (0, 0, 0)),
        scratch_shapes=[
            pltpu.VMEM((WL, 4, ROWS, K), BF16),
            pltpu.VMEM((WL, 2, ROWS, 128), F32),
            pltpu.VMEM((WL, 4, ROWS, BLK), F32),
            pltpu.VMEM((K + 8, ROWS), F32),
        ],
        compiler_params=pltpu.CompilerParams(vmem_limit_bytes=40 * 2**20),
        name="gradient",
    )(meta, x, tab, fld)


def fold(intensity, row):
    turned = jnp.where(row < 8, jnp.flip(intensity, axis=1), intensity)
    return jnp.concatenate(
        [turned[:, :, K + 1 :], turned[:, :, K : K + 1], jnp.flip(turned[:, :, :K], axis=2)], axis=2
    )


def local(phase, aperture, defocus_index, intensity):
    row = lax.axis_index("row")
    band = lax.axis_index("band")
    meta = jnp.concatenate(
        [jnp.stack([row, band * WL]).astype(jnp.int32), defocus_index.astype(jnp.int32)]
    )
    obs = fold(intensity, row)
    tab, fld, sent = run_forward(meta, phase, aperture)
    got = lax.all_to_all(sent, "row", 0, 0, tiled=True)
    sent = run_focal(got, tab, obs)
    got = lax.all_to_all(sent, "row", 0, 0, tiled=True)
    parts = run_gradient(meta, got, tab, fld)
    parts = lax.all_to_all(parts, "band", 0, 0, tiled=True)
    return jnp.sum(parts.astype(F32), axis=0)


def solution(mesh):
    return jax.shard_map(
        local,
        mesh=mesh,
        in_specs=(P("row", None), P("row", None), P("band"), P("band", "row", None)),
        out_specs=P("row", "band"),
        check_vma=False,
    )
```

```python
import math

import jax
import jax.numpy as jnp
from jax import lax
from jax.experimental import pallas as pl
from jax.experimental.pallas import tpu as pltpu
from jax.sharding import PartitionSpec as P

F32 = jnp.float32
BF16 = jnp.bfloat16
N = 4096
M = 512
HALF = N // 2
K = M // 2
ROWS = 256
BLK = 256
STEPS = HALF // BLK
WL = 2
GRP = 32
NORM = 1.0 / math.sqrt(N)

SIN_C = (9.99999246e-01, -1.66656827e-01, 8.31325871e-03, -1.85243573e-04)
COS_C = (9.99999953e-01, -4.99999053e-01, 4.16635847e-02, -1.38537043e-03, 2.31539316e-05)
SIN_T = (6.28318492, -41.34159016, 81.5999729, -76.61480386, 41.34439753, -12.47366849)
COS_T = (0.99999999, -19.73920453, 64.93911898, -85.45016555, 60.16783172, -25.96831326, 6.52961036)


def poly(coefs, y):
    acc = coefs[-1]
    for c in coefs[-2::-1]:
        acc = acc * y + c
    return acc


def turn(t):
    t = t - jnp.floor(t + 0.5)
    y = t * t
    return poly(COS_T, y), t * poly(SIN_T, y)


def unit(phi):
    y = phi * phi
    r2 = math.sqrt(2.0)
    c = poly([r2 * v / 4.0**n for n, v in enumerate(COS_C)], y)
    s = phi * poly([0.5 * r2 * v / 4.0**n for n, v in enumerate(SIN_C)], y)
    return c, s


def field(phi, amp):
    c, s = unit(phi)
    a_s = amp * s
    return amp - s * a_s, a_s * c


def lane_rev(x):
    rows, lanes = x.shape
    idx = 127 - lax.broadcasted_iota(jnp.int32, (rows, 128), 1)
    parts = [
        jnp.take_along_axis(x[:, s : s + 128], idx, axis=1, mode="promise_in_bounds")
        for s in range(lanes - 128, -1, -128)
    ]
    return jnp.concatenate(parts, axis=1) if len(parts) > 1 else parts[0]


def nt(a, b):
    return lax.dot_general(a, b, (((1,), (1,)), ((), ())), preferred_element_type=F32)


def nn(a, b):
    return lax.dot_general(a, b, (((1,), (0,)), ((), ())), preferred_element_type=F32)


def span(meta, w):
    return (1024 * (16 + meta[1] + w)).astype(F32)


def angle(n, m):
    inv = 1.0 / m
    q = jnp.floor(n * inv + 0.5)
    return turn((n - q * m) * inv)


def chirp_cols(meta, w, first, lanes):
    x = (2 * (first + lax.broadcasted_iota(jnp.int32, (1, lanes), 1)) + 1).astype(F32)
    return turn(x * x * (meta[2 + w].astype(F32) * (0.5 / (N * N))))


def chirp_rows(meta, w, row_pos):
    x = (2 * row_pos - (N - 1)).astype(F32)
    return turn(x * x * (meta[2 + w].astype(F32) * (0.5 / (N * N))))


def flip_matrix(flip):
    r = lax.broadcasted_iota(jnp.int32, (ROWS, ROWS), 0)
    c = lax.broadcasted_iota(jnp.int32, (ROWS, ROWS), 1)
    return jnp.where(jnp.where(flip, ROWS - 1 - c, c) == r, 1.0, 0.0).astype(BF16)


def forward_kernel(meta, ph_r, ph_l, ap_r, ap_l, tab, fld, out, z, rot, e_s, o_s, xacc, yacc, tmp):
    i = pl.program_id(0)

    @pl.when(i == 0)
    def _():
        xacc[...] = jnp.zeros_like(xacc)
        yacc[...] = jnp.zeros_like(yacc)
        for w in range(WL):
            m = span(meta, w)

            def init(t, _):
                r0 = pl.multiple_of(t * 32, 32)
                k = lax.broadcasted_iota(jnp.int32, (32, BLK), 0) + (r0 + 1)
                j = 2 * lax.broadcasted_iota(jnp.int32, (32, BLK), 1) + 1
                c, s = angle((k * j).astype(F32), m)
                z[w, 0, pl.ds(r0, 32), :] = c * NORM
                z[w, 1, pl.ds(r0, 32), :] = s * NORM
                k = lax.broadcasted_iota(jnp.int32, (32, 128), 0) + (r0 + 1)
                c, s = angle((k * (2 * BLK)).astype(F32), m)
                rot[w, 0, pl.ds(r0, 32), :] = c
                rot[w, 1, pl.ds(r0, 32), :] = s
                return 0

            lax.fori_loop(0, 8, init, 0)

    @pl.when(i > 0)
    def _():
        for w in range(WL):

            def step(t, _):
                r0 = pl.multiple_of(t * 32, 32)
                rc, rs = rot[w, 0, pl.ds(r0, 32), :], rot[w, 1, pl.ds(r0, 32), :]
                for h in (0, 128):
                    zc = z[w, 0, pl.ds(r0, 32), h : h + 128]
                    zs = z[w, 1, pl.ds(r0, 32), h : h + 128]
                    z[w, 0, pl.ds(r0, 32), h : h + 128] = zc * rc - zs * rs
                    z[w, 1, pl.ds(r0, 32), h : h + 128] = zc * rs + zs * rc
                return 0

            lax.fori_loop(0, 8, step, 0)

    dx = [chirp_cols(meta, w, i * BLK, BLK) for w in range(WL)]

    def rows(t, _):
        r0 = pl.multiple_of(t * 32, 32)
        sl = pl.ds(r0, 32)
        fr_c, fr_s = field(ph_r[sl, :], ap_r[sl, :].astype(F32))
        fl_c, fl_s = field(lane_rev(ph_l[sl, :]), lane_rev(ap_l[sl, :].astype(F32)))
        fld[0, sl, :] = fr_c
        fld[1, sl, :] = fr_s
        fld[2, sl, :] = fl_c
        fld[3, sl, :] = fl_s
        ec, es = fr_c + fl_c, fr_s + fl_s
        oc, os = fr_c - fl_c, fr_s - fl_s
        for w in range(WL):
            dc, ds = dx[w]
            e_s[w, 0, sl, :] = (ec * dc - es * ds).astype(BF16)
            e_s[w, 1, sl, :] = (ec * ds + es * dc).astype(BF16)
            o_s[w, 0, sl, :] = (oc * dc - os * ds).astype(BF16)
            o_s[w, 1, sl, :] = (oc * ds + os * dc).astype(BF16)
        return 0

    lax.fori_loop(0, ROWS // 32, rows, 0)
    ones = jnp.full((16, BLK), NORM, BF16)
    for w in range(WL):
        c = z[w, 0].astype(BF16)
        s = z[w, 1].astype(BF16)
        tab[w, 0] = c
        tab[w, 1] = s
        c = jnp.concatenate([c, ones], axis=0)
        for part in range(2):
            xacc[w, part] += nt(c, e_s[w, part])
            yacc[w, part] += nt(s, o_s[w, part])

    @pl.when(i == STEPS - 1)
    def _():
        row0 = meta[0] * ROWS
        j = flip_matrix(meta[0] < 8)
        pos = row0 + lax.broadcasted_iota(jnp.int32, (1, ROWS), 1)
        for w in range(WL):
            dc, ds = chirp_rows(meta, w, pos)
            xr, xi = xacc[w, 0], xacc[w, 1]
            yr, yi = yacc[w, 0], yacc[w, 1]
            xr, xi = xr * dc - xi * ds, xr * ds + xi * dc
            yr, yi = yr * dc - yi * ds, yr * ds + yi * dc
            x0 = (xr[K : K + 1], xi[K : K + 1])
            xr, xi = xr[:K], xi[:K]
            plus = (xr + yi, xi - yr)
            minus = (xr - yi, xi + yr)
            for part in range(2):
                tmp[pl.ds(8, K), :] = plus[part]
                tmp[pl.ds(7, 1), :] = x0[part]
                p = nn(tmp[pl.ds(7, K), :].astype(BF16), j).astype(BF16)
                m = nn(minus[part].astype(BF16), j).astype(BF16)
                at = (w * 2 + part) * GRP
                for g in range(8):
                    out[8 + g, at : at + GRP, :] = p[g * GRP : (g + 1) * GRP]
                    out[7 - g, at : at + GRP, :] = m[g * GRP : (g + 1) * GRP]


def focal_kernel(x, tab, obs, out):
    last = lax.broadcasted_iota(jnp.int32, (GRP, K), 1) == K - 1
    for w in range(WL):
        at = w * 2 * GRP
        acc_c = jnp.zeros((2 * GRP, K), F32)
        acc_s = jnp.zeros((2 * GRP, K), F32)
        centre = jnp.zeros((2 * GRP, BLK), F32)
        for i in range(STEPS):
            r = x[8 + i, at : at + 2 * GRP, :].astype(F32)
            l = x[7 - i, at : at + 2 * GRP, :].astype(F32)
            e = r + l
            centre = centre + e
            cols = slice(i * BLK, (i + 1) * BLK)
            acc_c = acc_c + nt(e.astype(BF16), tab[w, 0, :, cols])
            acc_s = acc_s + nt((r - l).astype(BF16), tab[w, 1, :, cols])
        centre = jnp.sum(centre, axis=1, keepdims=True) * NORM
        cr, ci = acc_c[:GRP], acc_c[GRP:]
        sr, si = acc_s[:GRP], acc_s[GRP:]
        weighted = []
        for side, (fr, fi) in enumerate(
            (
                (jnp.where(last, centre[:GRP], cr + si), jnp.where(last, centre[GRP:], ci - sr)),
                (cr - si, ci + sr),
            )
        ):
            misfit = fr * fr + fi * fi - obs[w, :, side * K : (side + 1) * K]
            weighted.append(
                [(misfit * fr).astype(BF16).astype(F32), (misfit * fi).astype(BF16).astype(F32)]
            )
        (pr, pi), (mr, mi) = weighted
        centre = jnp.concatenate([pr[:, K - 1 :], pi[:, K - 1 :]], axis=0) * NORM
        p = jnp.concatenate([jnp.where(last, 0.0, pr), jnp.where(last, 0.0, pi)], axis=0)
        m = jnp.concatenate([mr, mi], axis=0)
        s = (p + m).astype(BF16)
        d = (p - m).astype(BF16)
        for i in range(STEPS):
            cols = slice(i * BLK, (i + 1) * BLK)
            bc = nn(s, tab[w, 0, :, cols]) + centre
            bs = nn(d, tab[w, 1, :, cols])
            bcr, bci, bsr, bsi = bc[:GRP], bc[GRP:], bs[:GRP], bs[GRP:]
            out[8 + i, at : at + GRP, :] = (bcr - bsi).astype(BF16)
            out[8 + i, at + GRP : at + 2 * GRP, :] = (bci + bsr).astype(BF16)
            out[7 - i, at : at + GRP, :] = (bcr + bsi).astype(BF16)
            out[7 - i, at + GRP : at + 2 * GRP, :] = (bci - bsr).astype(BF16)


def gradient_kernel(meta, x, tab, fld, out, lhs, mid, sp, tmp):
    i = pl.program_id(0)

    @pl.when(i == 0)
    def _():
        flip = meta[0] < 8
        j = flip_matrix(flip)
        lane = lax.broadcasted_iota(jnp.int32, (1, ROWS), 1)
        pos = meta[0] * ROWS + jnp.where(flip, ROWS - 1 - lane, lane)
        for w in range(WL):
            dc, ds = chirp_rows(meta, w, pos)
            p, m, b0 = [], [], []
            for part in range(2):
                at = (w * 2 + part) * GRP
                for g in range(8):
                    tmp[g * GRP : (g + 1) * GRP, :] = x[8 + g, at : at + GRP, :].astype(F32)
                tmp[K : K + 8, :] = jnp.zeros((8, ROWS), F32)
                b0.append(tmp[0:1, :])
                p.append(tmp[pl.ds(1, K), :])
                m.append(
                    jnp.concatenate([x[7 - g, at : at + GRP, :] for g in range(8)], axis=0).astype(F32)
                )
            for n, (re, im) in enumerate(
                ((p[0] + m[0], p[1] + m[1]), (p[0] - m[0], p[1] - m[1]))
            ):
                lhs[w, 2 * n] = nt(j, (re * dc + im * ds).astype(BF16)).astype(BF16)
                lhs[w, 2 * n + 1] = nt(j, (im * dc - re * ds).astype(BF16)).astype(BF16)
            for part, v in enumerate((b0[0] * dc + b0[1] * ds, b0[1] * dc - b0[0] * ds)):
                v = jnp.broadcast_to((v * NORM).astype(BF16), (128, ROWS))
                mid[w, part] = nt(j, v)

    for w in range(WL):
        c = tab[w, 0]
        s = tab[w, 1]
        for part in range(2):
            sp[w, part] = nn(lhs[w, part], c)
            sp[w, 2 + part] = nn(lhs[w, 2 + part], s)
    dx = [chirp_cols(meta, w, i * BLK, BLK) for w in range(WL)]
    right = 4 + i // 2, pl.multiple_of((i % 2) * BLK, BLK)
    left = 3 - i // 2, pl.multiple_of((1 - i % 2) * BLK, BLK)

    def rows(t, _):
        r0 = pl.multiple_of(t * 32, 32)
        sl = pl.ds(r0, 32)
        tot = [0.0, 0.0, 0.0, 0.0]
        for w in range(WL):
            dc, ds = dx[w]
            m = [jnp.concatenate([mid[w, part, sl, :]] * 2, axis=1) for part in range(2)]
            cr, ci = sp[w, 0, sl, :] + m[0], sp[w, 1, sl, :] + m[1]
            sr, si = sp[w, 2, sl, :], sp[w, 3, sl, :]
            tot[0] += cr * dc + ci * ds
            tot[1] += ci * dc - cr * ds
            tot[2] += sr * dc + si * ds
            tot[3] += si * dc - sr * ds
        cr, ci, sr, si = tot
        g_r = (ci + sr) * fld[0, sl, :] - (cr - si) * fld[1, sl, :]
        g_l = (ci - sr) * fld[2, sl, :] - (cr + si) * fld[3, sl, :]
        out[right[0], sl, pl.ds(right[1], BLK)] = g_r.astype(BF16)
        out[left[0], sl, pl.ds(left[1], BLK)] = lane_rev(g_l).astype(BF16)
        return 0

    lax.fori_loop(0, ROWS // 32, rows, 0)


def run_forward(meta, phase, aperture):
    smem = pl.BlockSpec(memory_space=pltpu.SMEM)
    right = pl.BlockSpec((ROWS, BLK), lambda i: (0, STEPS + i))
    left = pl.BlockSpec((ROWS, BLK), lambda i: (0, STEPS - 1 - i))
    return pl.pallas_call(
        forward_kernel,
        grid=(STEPS,),
        out_shape=(
            jax.ShapeDtypeStruct((WL, 2, K, HALF), BF16),
            jax.ShapeDtypeStruct((4, ROWS, HALF), F32),
            jax.ShapeDtypeStruct((16, WL * 2 * GRP, ROWS), BF16),
        ),
        in_specs=[smem, right, left, right, left],
        out_specs=(
            pl.BlockSpec((WL, 2, K, BLK), lambda i: (0, 0, 0, i)),
            pl.BlockSpec((4, ROWS, BLK), lambda i: (0, 0, i)),
            pl.BlockSpec((16, WL * 2 * GRP, ROWS), lambda i: (0, 0, 0)),
        ),
        scratch_shapes=[
            pltpu.VMEM((WL, 2, K, BLK), F32),
            pltpu.VMEM((WL, 2, K, 128), F32),
            pltpu.VMEM((WL, 2, ROWS, BLK), BF16),
            pltpu.VMEM((WL, 2, ROWS, BLK), BF16),
            pltpu.VMEM((WL, 2, K + 16, ROWS), F32),
            pltpu.VMEM((WL, 2, K, ROWS), F32),
            pltpu.VMEM((K + 16, ROWS), F32),
        ],
        compiler_params=pltpu.CompilerParams(vmem_limit_bytes=60 * 2**20),
        name="forward",
    )(meta, phase, phase, aperture, aperture)


def run_focal(x, tab, obs):
    return pl.pallas_call(
        focal_kernel,
        out_shape=jax.ShapeDtypeStruct((16, WL * 2 * GRP, ROWS), BF16),
        in_specs=[pl.BlockSpec(memory_space=pltpu.VMEM)] * 3,
        out_specs=pl.BlockSpec(memory_space=pltpu.VMEM),
        compiler_params=pltpu.CompilerParams(vmem_limit_bytes=60 * 2**20),
        name="focal",
    )(x, tab, obs)


def run_gradient(meta, x, tab, fld):
    return pl.pallas_call(
        gradient_kernel,
        grid=(STEPS,),
        out_shape=jax.ShapeDtypeStruct((8, ROWS, M), BF16),
        in_specs=[
            pl.BlockSpec(memory_space=pltpu.SMEM),
            pl.BlockSpec((16, WL * 2 * GRP, ROWS), lambda i: (0, 0, 0)),
            pl.BlockSpec((WL, 2, K, BLK), lambda i: (0, 0, 0, i)),
            pl.BlockSpec((4, ROWS, BLK), lambda i: (0, 0, i)),
        ],
        out_specs=pl.BlockSpec((8, ROWS, M), lambda i: (0, 0, 0)),
        scratch_shapes=[
            pltpu.VMEM((WL, 4, ROWS, K), BF16),
            pltpu.VMEM((WL, 2, ROWS, 128), F32),
            pltpu.VMEM((WL, 4, ROWS, BLK), F32),
            pltpu.VMEM((K + 8, ROWS), F32),
        ],
        compiler_params=pltpu.CompilerParams(vmem_limit_bytes=60 * 2**20),
        name="gradient",
    )(meta, x, tab, fld)


def fold(intensity, row):
    turned = jnp.where(row < 8, jnp.flip(intensity, axis=1), intensity)
    return jnp.concatenate(
        [turned[:, :, K + 1 :], turned[:, :, K : K + 1], jnp.flip(turned[:, :, :K], axis=2)], axis=2
    )


def local(phase, aperture, defocus_index, intensity):
    row = lax.axis_index("row")
    band = lax.axis_index("band")
    meta = jnp.concatenate(
        [jnp.stack([row, band * WL]).astype(jnp.int32), defocus_index.astype(jnp.int32)]
    )
    obs, meta = lax.optimization_barrier((fold(intensity, row), meta))
    tab, fld, sent = run_forward(meta, phase, aperture)
    got = lax.all_to_all(sent, "row", 0, 0, tiled=True)
    sent = run_focal(got, tab, obs)
    got = lax.all_to_all(sent, "row", 0, 0, tiled=True)
    parts = run_gradient(meta, got, tab, fld)
    parts = lax.all_to_all(parts, "band", 0, 0, tiled=True)
    return jnp.sum(parts.astype(F32), axis=0)


def solution(mesh):
    return jax.shard_map(
        local,
        mesh=mesh,
        in_specs=(P("row", None), P("row", None), P("band"), P("band", "row", None)),
        out_specs=P("row", "band"),
        check_vma=False,
    )
```

```python
import math

import jax
import jax.numpy as jnp
from jax import lax
from jax.experimental import pallas as pl
from jax.experimental.pallas import tpu as pltpu
from jax.sharding import PartitionSpec as P

F32 = jnp.float32
BF16 = jnp.bfloat16
N = 4096
M = 512
HALF = N // 2
K = M // 2
ROWS = 256
BLK = 256
CB = 512
SUB = 256
CHUNK = 32
STEPS = HALF // BLK
WL = 2
GRP = 32
NORM = 1.0 / math.sqrt(N)

SIN_C = (9.99999246e-01, -1.66656827e-01, 8.31325871e-03, -1.85243573e-04)
COS_C = (9.99999953e-01, -4.99999053e-01, 4.16635847e-02, -1.38537043e-03, 2.31539316e-05)
SIN_T = (6.28318492, -41.34159016, 81.5999729, -76.61480386, 41.34439753, -12.47366849)
COS_T = (0.99999999, -19.73920453, 64.93911898, -85.45016555, 60.16783172, -25.96831326, 6.52961036)


def poly(coefs, y):
    acc = coefs[-1]
    for c in coefs[-2::-1]:
        acc = acc * y + c
    return acc


def turn(t):
    t = t - jnp.floor(t + 0.5)
    y = t * t
    return poly(COS_T, y), t * poly(SIN_T, y)


def unit(phi):
    y = phi * phi
    r2 = math.sqrt(2.0)
    c = poly([r2 * v / 4.0**n for n, v in enumerate(COS_C)], y)
    s = phi * poly([0.5 * r2 * v / 4.0**n for n, v in enumerate(SIN_C)], y)
    return c, s


def field(phi, amp):
    c, s = unit(phi)
    a_s = amp * s
    return amp - s * a_s, a_s * c


def lane_rev(x):
    rows, lanes = x.shape
    idx = 127 - lax.broadcasted_iota(jnp.int32, (rows, 128), 1)
    parts = [
        jnp.take_along_axis(x[:, s : s + 128], idx, axis=1, mode="promise_in_bounds")
        for s in range(lanes - 128, -1, -128)
    ]
    return jnp.concatenate(parts, axis=1) if len(parts) > 1 else parts[0]


def nt(a, b):
    return lax.dot_general(a, b, (((1,), (1,)), ((), ())), preferred_element_type=F32)


def nn(a, b):
    return lax.dot_general(a, b, (((1,), (0,)), ((), ())), preferred_element_type=F32)


def span(w):
    return (1024 * (16 + lax.axis_index("band") * WL + w)).astype(F32)


def angle(n, m):
    inv = 1.0 / m
    q = jnp.floor(n * inv + 0.5)
    return turn((n - q * m) * inv)


def chirp_cols(level, first, lanes):
    x = (2 * (first + lax.broadcasted_iota(jnp.int32, (1, lanes), 1)) + 1).astype(F32)
    return turn(x * x * (level.astype(F32) * (0.5 / (N * N))))


def chirp_rows(level, row_pos):
    x = (2 * row_pos - (N - 1)).astype(F32)
    return turn(x * x * (level.astype(F32) * (0.5 / (N * N))))


def flip_matrix(flip):
    r = lax.broadcasted_iota(jnp.int32, (ROWS, ROWS), 0)
    c = lax.broadcasted_iota(jnp.int32, (ROWS, ROWS), 1)
    return jnp.where(jnp.where(flip, ROWS - 1 - c, c) == r, 1.0, 0.0).astype(BF16)


def write_tables(tab, first):
    k = lax.broadcasted_iota(jnp.int32, (8, 128), 0) + 1
    lane = lax.broadcasted_iota(jnp.int32, (8, 128), 1)
    at, state = [], []
    for w in range(WL):
        m = span(w)
        for t in range(0, CB, 128):
            x = 2 * (first + t + lane) + 1
            c, s = angle((x * k).astype(F32), m)
            rc, rs = angle((x * 8).astype(F32), m)
            at.append((w, t))
            state.append((c * NORM, s * NORM, rc, rs))
    for q in range(K // 16):
        for n, (w, t) in enumerate(at):
            c0, s0, rc, rs = state[n]
            c1, s1 = c0 * rc - s0 * rs, c0 * rs + s0 * rc
            rows, lanes = slice(16 * q, 16 * q + 16), slice(t, t + 128)
            tab[w, 0, rows, lanes] = jnp.concatenate([c0, c1], axis=0).astype(BF16)
            tab[w, 1, rows, lanes] = jnp.concatenate([s0, s1], axis=0).astype(BF16)
            state[n] = (c1 * rc - s1 * rs, c1 * rs + s1 * rc, rc, rs)


def forward_kernel(level, ph_r, ph_l, ap_r, ap_l, tab, fld, out, e_s, o_s, xacc, yacc, tmp):
    i = pl.program_id(0)
    row = lax.axis_index("row")

    @pl.when(i == 0)
    def _():
        xacc[...] = jnp.zeros_like(xacc)
        yacc[...] = jnp.zeros_like(yacc)

    write_tables(tab, i * CB)
    dx = [chirp_cols(level[w], i * CB, CB) for w in range(WL)]
    ones = jnp.full((16, SUB), NORM, BF16)
    for h in range(0, CB, SUB):
        cols = slice(h, h + SUB)
        mirror = slice(CB - SUB - h, CB - h)
        for r0 in range(0, ROWS, CHUNK):
            sl = slice(r0, r0 + CHUNK)
            fr_c, fr_s = field(ph_r[sl, cols], ap_r[sl, cols].astype(F32))
            fl_c, fl_s = field(lane_rev(ph_l[sl, mirror]), lane_rev(ap_l[sl, mirror]).astype(F32))
            fld[0, sl, cols] = fr_c
            fld[1, sl, cols] = fr_s
            fld[2, sl, cols] = fl_c
            fld[3, sl, cols] = fl_s
            ec, es = fr_c + fl_c, fr_s + fl_s
            oc, os = fr_c - fl_c, fr_s - fl_s
            for w in range(WL):
                dc, ds = dx[w][0][:, cols], dx[w][1][:, cols]
                e_s[w, 0, sl, cols] = (ec * dc - es * ds).astype(BF16)
                e_s[w, 1, sl, cols] = (ec * ds + es * dc).astype(BF16)
                o_s[w, 0, sl, cols] = (oc * dc - os * ds).astype(BF16)
                o_s[w, 1, sl, cols] = (oc * ds + os * dc).astype(BF16)
        for w in range(WL):
            c = jnp.concatenate([tab[w, 0, :, cols], ones], axis=0)
            s = tab[w, 1, :, cols]
            for part in range(2):
                xacc[w, part] += nt(c, e_s[w, part, :, cols])
                yacc[w, part] += nt(s, o_s[w, part, :, cols])

    @pl.when(i == HALF // CB - 1)
    def _():
        j = flip_matrix(row < 8)
        pos = row * ROWS + lax.broadcasted_iota(jnp.int32, (1, ROWS), 1)
        for w in range(WL):
            dc, ds = chirp_rows(level[w], pos)
            xr, xi = xacc[w, 0], xacc[w, 1]
            yr, yi = yacc[w, 0], yacc[w, 1]
            xr, xi = xr * dc - xi * ds, xr * ds + xi * dc
            yr, yi = yr * dc - yi * ds, yr * ds + yi * dc
            x0 = (xr[K : K + 1], xi[K : K + 1])
            xr, xi = xr[:K], xi[:K]
            plus = (xr + yi, xi - yr)
            minus = (xr - yi, xi + yr)
            for part in range(2):
                tmp[pl.ds(8, K), :] = plus[part]
                tmp[pl.ds(7, 1), :] = x0[part]
                p = nn(tmp[pl.ds(7, K), :].astype(BF16), j).astype(BF16)
                m = nn(minus[part].astype(BF16), j).astype(BF16)
                at = (w * 2 + part) * GRP
                for g in range(8):
                    out[8 + g, at : at + GRP, :] = p[g * GRP : (g + 1) * GRP]
                    out[7 - g, at : at + GRP, :] = m[g * GRP : (g + 1) * GRP]


def focal_kernel(x, tab, seen, out, obs):
    low = lax.axis_index("row") < 8
    for w in range(WL):
        for r in range(GRP):
            obs[w, pl.ds(jnp.where(low, GRP - 1 - r, r), 1), :] = seen[w, r : r + 1, :]
    last = lax.broadcasted_iota(jnp.int32, (GRP, K), 1) == K - 1
    for w in range(WL):
        at = w * 2 * GRP
        acc_c = jnp.zeros((2 * GRP, K), F32)
        acc_s = jnp.zeros((2 * GRP, K), F32)
        centre = jnp.zeros((2 * GRP, BLK), F32)
        for i in range(STEPS):
            r = x[8 + i, at : at + 2 * GRP, :].astype(F32)
            l = x[7 - i, at : at + 2 * GRP, :].astype(F32)
            e = r + l
            centre = centre + e
            cols = slice(i * BLK, (i + 1) * BLK)
            acc_c = acc_c + nt(e.astype(BF16), tab[w, 0, :, cols])
            acc_s = acc_s + nt((r - l).astype(BF16), tab[w, 1, :, cols])
        centre = jnp.sum(centre, axis=1, keepdims=True) * NORM
        cr, ci = acc_c[:GRP], acc_c[GRP:]
        sr, si = acc_s[:GRP], acc_s[GRP:]
        rest = pltpu.roll(obs[w, :, K:], K - 1, 1)
        weighted = []
        for side, (fr, fi) in enumerate(
            (
                (jnp.where(last, centre[:GRP], cr + si), jnp.where(last, centre[GRP:], ci - sr)),
                (cr - si, ci + sr),
            )
        ):
            misfit = fr * fr + fi * fi - (rest if side == 0 else lane_rev(obs[w, :, :K]))
            weighted.append(
                [(misfit * fr).astype(BF16).astype(F32), (misfit * fi).astype(BF16).astype(F32)]
            )
        (pr, pi), (mr, mi) = weighted
        centre = jnp.concatenate([pr[:, K - 1 :], pi[:, K - 1 :]], axis=0) * NORM
        p = jnp.concatenate([jnp.where(last, 0.0, pr), jnp.where(last, 0.0, pi)], axis=0)
        m = jnp.concatenate([mr, mi], axis=0)
        s = (p + m).astype(BF16)
        d = (p - m).astype(BF16)
        for i in range(STEPS):
            cols = slice(i * BLK, (i + 1) * BLK)
            bc = nn(s, tab[w, 0, :, cols]) + centre
            bs = nn(d, tab[w, 1, :, cols])
            bcr, bci, bsr, bsi = bc[:GRP], bc[GRP:], bs[:GRP], bs[GRP:]
            out[8 + i, at : at + GRP, :] = (bcr - bsi).astype(BF16)
            out[8 + i, at + GRP : at + 2 * GRP, :] = (bci + bsr).astype(BF16)
            out[7 - i, at : at + GRP, :] = (bcr + bsi).astype(BF16)
            out[7 - i, at + GRP : at + 2 * GRP, :] = (bci - bsr).astype(BF16)


def gradient_kernel(level, x, tab, fld, out, lhs, mid, sp, tmp):
    i = pl.program_id(0)
    row = lax.axis_index("row")

    @pl.when(i == 0)
    def _():
        flip = row < 8
        j = flip_matrix(flip)
        lane = lax.broadcasted_iota(jnp.int32, (1, ROWS), 1)
        pos = row * ROWS + jnp.where(flip, ROWS - 1 - lane, lane)
        for w in range(WL):
            dc, ds = chirp_rows(level[w], pos)
            p, m, b0 = [], [], []
            for part in range(2):
                at = (w * 2 + part) * GRP
                for g in range(8):
                    tmp[g * GRP : (g + 1) * GRP, :] = x[8 + g, at : at + GRP, :].astype(F32)
                tmp[K : K + 8, :] = jnp.zeros((8, ROWS), F32)
                b0.append(tmp[0:1, :])
                p.append(tmp[pl.ds(1, K), :])
                m.append(
                    jnp.concatenate([x[7 - g, at : at + GRP, :] for g in range(8)], axis=0).astype(F32)
                )
            for n, (re, im) in enumerate(
                ((p[0] + m[0], p[1] + m[1]), (p[0] - m[0], p[1] - m[1]))
            ):
                lhs[w, 2 * n] = nt(j, (re * dc + im * ds).astype(BF16)).astype(BF16)
                lhs[w, 2 * n + 1] = nt(j, (im * dc - re * ds).astype(BF16)).astype(BF16)
            for part, v in enumerate((b0[0] * dc + b0[1] * ds, b0[1] * dc - b0[0] * ds)):
                v = jnp.broadcast_to((v * NORM).astype(BF16), (128, ROWS))
                mid[w, part] = nt(j, v)

    dx = [chirp_cols(level[w], i * CB, CB) for w in range(WL)]
    half = M // CB if CB < M else 1
    right = 4 + i * CB // M, pl.multiple_of(i % half * CB, CB)
    left = 3 - i * CB // M, pl.multiple_of((half - 1 - i % half) * CB, CB)
    for h in range(0, CB, SUB):
        cols = slice(h, h + SUB)
        for w in range(WL):
            for part in range(2):
                sp[w, part, :, cols] = nn(lhs[w, part], tab[w, 0, :, cols])
                sp[w, 2 + part, :, cols] = nn(lhs[w, 2 + part], tab[w, 1, :, cols])
        for r0 in range(0, ROWS, CHUNK):
            sl = slice(r0, r0 + CHUNK)
            tot = [0.0, 0.0, 0.0, 0.0]
            for w in range(WL):
                dc, ds = dx[w][0][:, cols], dx[w][1][:, cols]
                m = [jnp.concatenate([mid[w, part, sl, :]] * (SUB // 128), axis=1) for part in range(2)]
                cr, ci = sp[w, 0, sl, cols] + m[0], sp[w, 1, sl, cols] + m[1]
                sr, si = sp[w, 2, sl, cols], sp[w, 3, sl, cols]
                tot[0] += cr * dc + ci * ds
                tot[1] += ci * dc - cr * ds
                tot[2] += sr * dc + si * ds
                tot[3] += si * dc - sr * ds
            cr, ci, sr, si = tot
            g_r = (ci + sr) * fld[0, sl, cols] - (cr - si) * fld[1, sl, cols]
            g_l = (ci - sr) * fld[2, sl, cols] - (cr + si) * fld[3, sl, cols]
            out[right[0], sl, pl.ds(right[1] + h, SUB)] = g_r.astype(BF16)
            out[left[0], sl, pl.ds(left[1] + (CB - SUB - h), SUB)] = lane_rev(g_l).astype(BF16)


def run_forward(level, phase, aperture):
    smem = pl.BlockSpec(memory_space=pltpu.SMEM)
    right = pl.BlockSpec((ROWS, CB), lambda i: (0, HALF // CB + i))
    left = pl.BlockSpec((ROWS, CB), lambda i: (0, HALF // CB - 1 - i))
    return pl.pallas_call(
        forward_kernel,
        grid=(HALF // CB,),
        out_shape=(
            jax.ShapeDtypeStruct((WL, 2, K, HALF), BF16),
            jax.ShapeDtypeStruct((4, ROWS, HALF), F32),
            jax.ShapeDtypeStruct((16, WL * 2 * GRP, ROWS), BF16),
        ),
        in_specs=[smem, right, left, right, left],
        out_specs=(
            pl.BlockSpec((WL, 2, K, CB), lambda i: (0, 0, 0, i)),
            pl.BlockSpec((4, ROWS, CB), lambda i: (0, 0, i)),
            pl.BlockSpec((16, WL * 2 * GRP, ROWS), lambda i: (0, 0, 0)),
        ),
        scratch_shapes=[
            pltpu.VMEM((WL, 2, ROWS, CB), BF16),
            pltpu.VMEM((WL, 2, ROWS, CB), BF16),
            pltpu.VMEM((WL, 2, K + 16, ROWS), F32),
            pltpu.VMEM((WL, 2, K, ROWS), F32),
            pltpu.VMEM((K + 16, ROWS), F32),
        ],
        compiler_params=pltpu.CompilerParams(vmem_limit_bytes=60 * 2**20),
        name="forward",
    )(level, phase, phase, aperture, aperture)


def run_focal(x, tab, seen):
    return pl.pallas_call(
        focal_kernel,
        out_shape=jax.ShapeDtypeStruct((16, WL * 2 * GRP, ROWS), BF16),
        in_specs=[pl.BlockSpec(memory_space=pltpu.VMEM)] * 3,
        out_specs=pl.BlockSpec(memory_space=pltpu.VMEM),
        scratch_shapes=[pltpu.VMEM((WL, GRP, M), F32)],
        compiler_params=pltpu.CompilerParams(vmem_limit_bytes=60 * 2**20),
        name="focal",
    )(x, tab, seen)


def run_gradient(level, x, tab, fld):
    return pl.pallas_call(
        gradient_kernel,
        grid=(HALF // CB,),
        out_shape=jax.ShapeDtypeStruct((8, ROWS, M), BF16),
        in_specs=[
            pl.BlockSpec(memory_space=pltpu.SMEM),
            pl.BlockSpec((16, WL * 2 * GRP, ROWS), lambda i: (0, 0, 0)),
            pl.BlockSpec((WL, 2, K, CB), lambda i: (0, 0, 0, i)),
            pl.BlockSpec((4, ROWS, CB), lambda i: (0, 0, i)),
        ],
        out_specs=pl.BlockSpec((8, ROWS, M), lambda i: (0, 0, 0)),
        scratch_shapes=[
            pltpu.VMEM((WL, 4, ROWS, K), BF16),
            pltpu.VMEM((WL, 2, ROWS, 128), F32),
            pltpu.VMEM((WL, 4, ROWS, CB), F32),
            pltpu.VMEM((K + 8, ROWS), F32),
        ],
        compiler_params=pltpu.CompilerParams(vmem_limit_bytes=60 * 2**20),
        name="gradient",
    )(level, x, tab, fld)


def local(phase, aperture, defocus_index, intensity):
    level = defocus_index.astype(jnp.int32)
    tab, fld, sent = run_forward(level, phase, aperture)
    got = lax.all_to_all(sent, "row", 0, 0, tiled=True)
    sent = run_focal(got, tab, intensity)
    got = lax.all_to_all(sent, "row", 0, 0, tiled=True)
    parts = run_gradient(level, got, tab, fld)
    parts = lax.all_to_all(parts, "band", 0, 0, tiled=True)
    return jnp.sum(parts.astype(F32), axis=0)


def solution(mesh):
    return jax.shard_map(
        local,
        mesh=mesh,
        in_specs=(P("row", None), P("row", None), P("band"), P("band", "row", None)),
        out_specs=P("row", "band"),
        check_vma=False,
    )
```

```python
import math

import jax
import jax.numpy as jnp
from jax import lax
from jax.experimental import pallas as pl
from jax.experimental.pallas import tpu as pltpu
from jax.sharding import PartitionSpec as P

F32 = jnp.float32
BF16 = jnp.bfloat16
N = 4096
M = 512
HALF = N // 2
K = M // 2
ROWS = 256
BLK = 256
CB = 512
SUB = 256
CHUNK = 32
STEPS = HALF // BLK
WL = 2
GRP = 32
NORM = 1.0 / math.sqrt(N)

SIN_C = (9.99999246e-01, -1.66656827e-01, 8.31325871e-03, -1.85243573e-04)
COS_C = (9.99999953e-01, -4.99999053e-01, 4.16635847e-02, -1.38537043e-03, 2.31539316e-05)
SIN_T = (6.28318492, -41.34159016, 81.5999729, -76.61480386, 41.34439753, -12.47366849)
COS_T = (0.99999999, -19.73920453, 64.93911898, -85.45016555, 60.16783172, -25.96831326, 6.52961036)


def poly(coefs, y):
    acc = coefs[-1]
    for c in coefs[-2::-1]:
        acc = acc * y + c
    return acc


def turn(t):
    t = t - jnp.floor(t + 0.5)
    y = t * t
    return poly(COS_T, y), t * poly(SIN_T, y)


def unit(phi):
    y = phi * phi
    r2 = math.sqrt(2.0)
    c = poly([r2 * v / 4.0**n for n, v in enumerate(COS_C)], y)
    s = phi * poly([0.5 * r2 * v / 4.0**n for n, v in enumerate(SIN_C)], y)
    return c, s


def field(phi, amp):
    c, s = unit(phi)
    a_s = amp * s
    return amp - s * a_s, a_s * c


def lane_rev(x):
    rows, lanes = x.shape
    idx = 127 - lax.broadcasted_iota(jnp.int32, (rows, 128), 1)
    parts = [
        jnp.take_along_axis(x[:, s : s + 128], idx, axis=1, mode="promise_in_bounds")
        for s in range(lanes - 128, -1, -128)
    ]
    return jnp.concatenate(parts, axis=1) if len(parts) > 1 else parts[0]


def nt(a, b):
    return lax.dot_general(a, b, (((1,), (1,)), ((), ())), preferred_element_type=F32)


def nn(a, b):
    return lax.dot_general(a, b, (((1,), (0,)), ((), ())), preferred_element_type=F32)


def span(w):
    return (1024 * (16 + lax.axis_index("band") * WL + w)).astype(F32)


def angle(n, m):
    inv = 1.0 / m
    q = jnp.floor(n * inv + 0.5)
    return turn((n - q * m) * inv)


def chirp_cols(level, first, lanes):
    x = (2 * (first + lax.broadcasted_iota(jnp.int32, (1, lanes), 1)) + 1).astype(F32)
    return turn(x * x * (level.astype(F32) * (0.5 / (N * N))))


def chirp_rows(level, row_pos):
    x = (2 * row_pos - (N - 1)).astype(F32)
    return turn(x * x * (level.astype(F32) * (0.5 / (N * N))))


def flip_matrix(flip):
    r = lax.broadcasted_iota(jnp.int32, (ROWS, ROWS), 0)
    c = lax.broadcasted_iota(jnp.int32, (ROWS, ROWS), 1)
    return jnp.where(jnp.where(flip, ROWS - 1 - c, c) == r, 1.0, 0.0).astype(BF16)


def write_tables(tab, first):
    k = lax.broadcasted_iota(jnp.int32, (8, 128), 0) + 1
    lane = lax.broadcasted_iota(jnp.int32, (8, 128), 1)
    at, state = [], []
    for w in range(WL):
        m = span(w)
        for t in range(0, CB, 128):
            x = 2 * (first + t + lane) + 1
            c, s = angle((x * k).astype(F32), m)
            rc, rs = angle((x * 8).astype(F32), m)
            at.append((w, t))
            state.append((c * NORM, s * NORM, rc, rs))
    for q in range(K // 16):
        for n, (w, t) in enumerate(at):
            c0, s0, rc, rs = state[n]
            c1, s1 = c0 * rc - s0 * rs, c0 * rs + s0 * rc
            rows, lanes = slice(16 * q, 16 * q + 16), slice(t, t + 128)
            tab[w, 0, rows, lanes] = jnp.concatenate([c0, c1], axis=0).astype(BF16)
            tab[w, 1, rows, lanes] = jnp.concatenate([s0, s1], axis=0).astype(BF16)
            state[n] = (c1 * rc - s1 * rs, c1 * rs + s1 * rc, rc, rs)


def forward_kernel(level, ph_r, ph_l, ap_r, ap_l, tab, fld, out, e_s, o_s, xacc, yacc, tmp):
    i = pl.program_id(0)
    row = lax.axis_index("row")

    @pl.when(i == 0)
    def _():
        xacc[...] = jnp.zeros_like(xacc)
        yacc[...] = jnp.zeros_like(yacc)

    write_tables(tab, i * CB)
    dx = [chirp_cols(level[w], i * CB, CB) for w in range(WL)]
    ones = jnp.full((16, SUB), NORM, BF16)
    for h in range(0, CB, SUB):
        cols = slice(h, h + SUB)
        mirror = slice(CB - SUB - h, CB - h)
        for r0 in range(0, ROWS, CHUNK):
            sl = slice(r0, r0 + CHUNK)
            fr_c, fr_s = field(ph_r[sl, cols], ap_r[sl, cols].astype(F32))
            fl_c, fl_s = field(lane_rev(ph_l[sl, mirror]), lane_rev(ap_l[sl, mirror]).astype(F32))
            fld[0, sl, cols] = fr_c
            fld[1, sl, cols] = fr_s
            fld[2, sl, cols] = fl_c
            fld[3, sl, cols] = fl_s
            ec, es = fr_c + fl_c, fr_s + fl_s
            oc, os = fr_c - fl_c, fr_s - fl_s
            for w in range(WL):
                dc, ds = dx[w][0][:, cols], dx[w][1][:, cols]
                e_s[w, 0, sl, cols] = (ec * dc - es * ds).astype(BF16)
                e_s[w, 1, sl, cols] = (ec * ds + es * dc).astype(BF16)
                o_s[w, 0, sl, cols] = (oc * dc - os * ds).astype(BF16)
                o_s[w, 1, sl, cols] = (oc * ds + os * dc).astype(BF16)
        for w in range(WL):
            c = jnp.concatenate([tab[w, 0, :, cols], ones], axis=0)
            s = tab[w, 1, :, cols]
            for part in range(2):
                xacc[w, part] += nt(c, e_s[w, part, :, cols])
                yacc[w, part] += nt(s, o_s[w, part, :, cols])

    @pl.when(i == HALF // CB - 1)
    def _():
        j = flip_matrix(row < 8)
        pos = row * ROWS + lax.broadcasted_iota(jnp.int32, (1, ROWS), 1)
        for w in range(WL):
            dc, ds = chirp_rows(level[w], pos)
            xr, xi = xacc[w, 0], xacc[w, 1]
            yr, yi = yacc[w, 0], yacc[w, 1]
            xr, xi = xr * dc - xi * ds, xr * ds + xi * dc
            yr, yi = yr * dc - yi * ds, yr * ds + yi * dc
            x0 = (xr[K : K + 1], xi[K : K + 1])
            xr, xi = xr[:K], xi[:K]
            plus = (xr + yi, xi - yr)
            minus = (xr - yi, xi + yr)
            for part in range(2):
                tmp[pl.ds(8, K), :] = plus[part]
                tmp[pl.ds(7, 1), :] = x0[part]
                p = nn(tmp[pl.ds(7, K), :].astype(BF16), j).astype(BF16)
                m = nn(minus[part].astype(BF16), j).astype(BF16)
                at = (w * 2 + part) * GRP
                for g in range(8):
                    out[8 + g, at : at + GRP, :] = p[g * GRP : (g + 1) * GRP]
                    out[7 - g, at : at + GRP, :] = m[g * GRP : (g + 1) * GRP]


def focal_kernel(x, tab, seen, out, obs):
    low = lax.axis_index("row") < 8
    for w in range(WL):
        for r in range(GRP):
            obs[w, pl.ds(jnp.where(low, GRP - 1 - r, r), 1), :] = seen[w, r : r + 1, :]
    last = lax.broadcasted_iota(jnp.int32, (GRP, K), 1) == K - 1
    for w in range(WL):
        at = w * 2 * GRP
        acc_c = jnp.zeros((2 * GRP, K), F32)
        acc_s = jnp.zeros((2 * GRP, K), F32)
        centre = jnp.zeros((2 * GRP, BLK), F32)
        for i in range(STEPS):
            r = x[8 + i, at : at + 2 * GRP, :].astype(F32)
            l = x[7 - i, at : at + 2 * GRP, :].astype(F32)
            e = r + l
            centre = centre + e
            cols = slice(i * BLK, (i + 1) * BLK)
            acc_c = acc_c + nt(e.astype(BF16), tab[w, 0, :, cols])
            acc_s = acc_s + nt((r - l).astype(BF16), tab[w, 1, :, cols])
        centre = jnp.sum(centre, axis=1, keepdims=True) * NORM
        cr, ci = acc_c[:GRP], acc_c[GRP:]
        sr, si = acc_s[:GRP], acc_s[GRP:]
        rest = pltpu.roll(obs[w, :, K:], K - 1, 1)
        weighted = []
        for side, (fr, fi) in enumerate(
            (
                (jnp.where(last, centre[:GRP], cr + si), jnp.where(last, centre[GRP:], ci - sr)),
                (cr - si, ci + sr),
            )
        ):
            misfit = fr * fr + fi * fi - (rest if side == 0 else lane_rev(obs[w, :, :K]))
            weighted.append(
                [(misfit * fr).astype(BF16).astype(F32), (misfit * fi).astype(BF16).astype(F32)]
            )
        (pr, pi), (mr, mi) = weighted
        centre = jnp.concatenate([pr[:, K - 1 :], pi[:, K - 1 :]], axis=0) * NORM
        p = jnp.concatenate([jnp.where(last, 0.0, pr), jnp.where(last, 0.0, pi)], axis=0)
        m = jnp.concatenate([mr, mi], axis=0)
        s = (p + m).astype(BF16)
        d = (p - m).astype(BF16)
        for i in range(STEPS):
            cols = slice(i * BLK, (i + 1) * BLK)
            bc = nn(s, tab[w, 0, :, cols]) + centre
            bs = nn(d, tab[w, 1, :, cols])
            bcr, bci, bsr, bsi = bc[:GRP], bc[GRP:], bs[:GRP], bs[GRP:]
            out[8 + i, at : at + GRP, :] = (bcr - bsi).astype(BF16)
            out[8 + i, at + GRP : at + 2 * GRP, :] = (bci + bsr).astype(BF16)
            out[7 - i, at : at + GRP, :] = (bcr + bsi).astype(BF16)
            out[7 - i, at + GRP : at + 2 * GRP, :] = (bci - bsr).astype(BF16)


def gradient_kernel(level, x, tab, fld, out, lhs, mid, sp, tmp):
    row = lax.axis_index("row")
    flip = row < 8
    j = flip_matrix(flip)
    lane = lax.broadcasted_iota(jnp.int32, (1, ROWS), 1)
    pos = row * ROWS + jnp.where(flip, ROWS - 1 - lane, lane)
    for w in range(WL):
        dc, ds = chirp_rows(level[w], pos)
        p, m, b0 = [], [], []
        for part in range(2):
            at = (w * 2 + part) * GRP
            for g in range(8):
                tmp[g * GRP : (g + 1) * GRP, :] = x[8 + g, at : at + GRP, :].astype(F32)
            tmp[K : K + 8, :] = jnp.zeros((8, ROWS), F32)
            b0.append(tmp[0:1, :])
            p.append(tmp[pl.ds(1, K), :])
            m.append(
                jnp.concatenate([x[7 - g, at : at + GRP, :] for g in range(8)], axis=0).astype(F32)
            )
        for n, (re, im) in enumerate(
            ((p[0] + m[0], p[1] + m[1]), (p[0] - m[0], p[1] - m[1]))
        ):
            lhs[w, 2 * n] = nt(j, (re * dc + im * ds).astype(BF16)).astype(BF16)
            lhs[w, 2 * n + 1] = nt(j, (im * dc - re * ds).astype(BF16)).astype(BF16)
        for part, v in enumerate((b0[0] * dc + b0[1] * ds, b0[1] * dc - b0[0] * ds)):
            v = jnp.broadcast_to((v * NORM).astype(BF16), (128, ROWS))
            mid[w, part] = nt(j, v)

    def block(i, _):
        base = pl.multiple_of(i * CB, CB)
        dx = [chirp_cols(level[w], base, CB) for w in range(WL)]
        per = M // CB
        right = 4 + i // per, pl.multiple_of(i % per * CB, CB)
        left = 3 - i // per, pl.multiple_of((per - 1 - i % per) * CB, CB)
        for h in range(0, CB, SUB):
            cols = pl.ds(pl.multiple_of(base + h, SUB), SUB)
            for w in range(WL):
                for part in range(2):
                    sp[w, part, :, h : h + SUB] = nn(lhs[w, part], tab[w, 0, :, cols])
                    sp[w, 2 + part, :, h : h + SUB] = nn(lhs[w, 2 + part], tab[w, 1, :, cols])
            for r0 in range(0, ROWS, CHUNK):
                sl = slice(r0, r0 + CHUNK)
                tot = [0.0, 0.0, 0.0, 0.0]
                for w in range(WL):
                    dc, ds = dx[w][0][:, h : h + SUB], dx[w][1][:, h : h + SUB]
                    m = [
                        jnp.concatenate([mid[w, part, sl, :]] * (SUB // 128), axis=1)
                        for part in range(2)
                    ]
                    cr, ci = sp[w, 0, sl, h : h + SUB] + m[0], sp[w, 1, sl, h : h + SUB] + m[1]
                    sr, si = sp[w, 2, sl, h : h + SUB], sp[w, 3, sl, h : h + SUB]
                    tot[0] += cr * dc + ci * ds
                    tot[1] += ci * dc - cr * ds
                    tot[2] += sr * dc + si * ds
                    tot[3] += si * dc - sr * ds
                cr, ci, sr, si = tot
                g_r = (ci + sr) * fld[0, sl, cols] - (cr - si) * fld[1, sl, cols]
                g_l = (ci - sr) * fld[2, sl, cols] - (cr + si) * fld[3, sl, cols]
                out[right[0], sl, pl.ds(right[1] + h, SUB)] = g_r.astype(BF16)
                out[left[0], sl, pl.ds(left[1] + (CB - SUB - h), SUB)] = lane_rev(g_l).astype(BF16)
        return 0

    lax.fori_loop(0, HALF // CB, block, 0)


def run_forward(level, phase, aperture):
    smem = pl.BlockSpec(memory_space=pltpu.SMEM)
    right = pl.BlockSpec((ROWS, CB), lambda i: (0, HALF // CB + i))
    left = pl.BlockSpec((ROWS, CB), lambda i: (0, HALF // CB - 1 - i))
    return pl.pallas_call(
        forward_kernel,
        grid=(HALF // CB,),
        out_shape=(
            jax.ShapeDtypeStruct((WL, 2, K, HALF), BF16),
            jax.ShapeDtypeStruct((4, ROWS, HALF), F32),
            jax.ShapeDtypeStruct((16, WL * 2 * GRP, ROWS), BF16),
        ),
        in_specs=[smem, right, left, right, left],
        out_specs=(
            pl.BlockSpec((WL, 2, K, CB), lambda i: (0, 0, 0, i)),
            pl.BlockSpec((4, ROWS, CB), lambda i: (0, 0, i)),
            pl.BlockSpec((16, WL * 2 * GRP, ROWS), lambda i: (0, 0, 0)),
        ),
        scratch_shapes=[
            pltpu.VMEM((WL, 2, ROWS, CB), BF16),
            pltpu.VMEM((WL, 2, ROWS, CB), BF16),
            pltpu.VMEM((WL, 2, K + 16, ROWS), F32),
            pltpu.VMEM((WL, 2, K, ROWS), F32),
            pltpu.VMEM((K + 16, ROWS), F32),
        ],
        compiler_params=pltpu.CompilerParams(vmem_limit_bytes=60 * 2**20),
        name="forward",
    )(level, phase, phase, aperture, aperture)


def run_focal(x, tab, seen):
    return pl.pallas_call(
        focal_kernel,
        out_shape=jax.ShapeDtypeStruct((16, WL * 2 * GRP, ROWS), BF16),
        in_specs=[pl.BlockSpec(memory_space=pltpu.VMEM)] * 3,
        out_specs=pl.BlockSpec(memory_space=pltpu.VMEM),
        scratch_shapes=[pltpu.VMEM((WL, GRP, M), F32)],
        compiler_params=pltpu.CompilerParams(vmem_limit_bytes=20 * 2**20),
        cost_estimate=pl.CostEstimate(flops=2**34, bytes_accessed=2**26, transcendentals=0),
        name="focal",
    )(x, tab, seen)


def run_gradient(level, x, tab, fld):
    return pl.pallas_call(
        gradient_kernel,
        out_shape=jax.ShapeDtypeStruct((8, ROWS, M), BF16),
        in_specs=[pl.BlockSpec(memory_space=pltpu.SMEM)] + [pl.BlockSpec(memory_space=pltpu.VMEM)] * 3,
        out_specs=pl.BlockSpec(memory_space=pltpu.VMEM),
        scratch_shapes=[
            pltpu.VMEM((WL, 4, ROWS, K), BF16),
            pltpu.VMEM((WL, 2, ROWS, 128), F32),
            pltpu.VMEM((WL, 4, ROWS, CB), F32),
            pltpu.VMEM((K + 8, ROWS), F32),
        ],
        compiler_params=pltpu.CompilerParams(vmem_limit_bytes=28 * 2**20),
        cost_estimate=pl.CostEstimate(flops=2**34, bytes_accessed=2**26, transcendentals=0),
        name="gradient",
    )(level, x, tab, fld)


def local(phase, aperture, defocus_index, intensity):
    level = defocus_index.astype(jnp.int32)
    tab, fld, sent = run_forward(level, phase, aperture)
    got = lax.all_to_all(sent, "row", 0, 0, tiled=True)
    sent = run_focal(got, tab, intensity)
    got = lax.all_to_all(sent, "row", 0, 0, tiled=True)
    parts = run_gradient(level, got, tab, fld)
    parts = lax.all_to_all(parts, "band", 0, 0, tiled=True)
    return jnp.sum(parts.astype(F32), axis=0)


def solution(mesh):
    return jax.shard_map(
        local,
        mesh=mesh,
        in_specs=(P("row", None), P("row", None), P("band"), P("band", "row", None)),
        out_specs=P("row", "band"),
        check_vma=False,
    )
```

```python
import math

import jax
import jax.numpy as jnp
from jax import lax
from jax.experimental import pallas as pl
from jax.experimental.pallas import tpu as pltpu
from jax.sharding import Mesh
from jax.sharding import PartitionSpec as P

F32 = jnp.float32
BF16 = jnp.bfloat16
N = 4096
M = 512
HALF = N // 2
K = M // 2
ROWS = 256
BLK = 256
CB = 512
SUB = 256
CHUNK = 32
STEPS = HALF // BLK
WL = 2
GRP = 32
PAIR = 2
PART = ROWS // PAIR
NORM = 1.0 / math.sqrt(N)

SIN_C = (9.99999246e-01, -1.66656827e-01, 8.31325871e-03, -1.85243573e-04)
COS_C = (9.99999953e-01, -4.99999053e-01, 4.16635847e-02, -1.38537043e-03, 2.31539316e-05)
SIN_T = (6.28318492, -41.34159016, 81.5999729, -76.61480386, 41.34439753, -12.47366849)
COS_T = (0.99999999, -19.73920453, 64.93911898, -85.45016555, 60.16783172, -25.96831326, 6.52961036)


def poly(coefs, y):
    acc = coefs[-1]
    for c in coefs[-2::-1]:
        acc = acc * y + c
    return acc


def turn(t):
    t = t - jnp.floor(t + 0.5)
    y = t * t
    return poly(COS_T, y), t * poly(SIN_T, y)


def unit(phi):
    y = phi * phi
    r2 = math.sqrt(2.0)
    c = poly([r2 * v / 4.0**n for n, v in enumerate(COS_C)], y)
    s = phi * poly([0.5 * r2 * v / 4.0**n for n, v in enumerate(SIN_C)], y)
    return c, s


def field(phi, amp):
    c, s = unit(phi)
    a_s = amp * s
    return amp - s * a_s, a_s * c


def lane_rev(x):
    rows, lanes = x.shape
    idx = 127 - lax.broadcasted_iota(jnp.int32, (rows, 128), 1)
    parts = [
        jnp.take_along_axis(x[:, s : s + 128], idx, axis=1, mode="promise_in_bounds")
        for s in range(lanes - 128, -1, -128)
    ]
    return jnp.concatenate(parts, axis=1) if len(parts) > 1 else parts[0]


def nt(a, b):
    return lax.dot_general(a, b, (((1,), (1,)), ((), ())), preferred_element_type=F32)


def nn(a, b):
    return lax.dot_general(a, b, (((1,), (0,)), ((), ())), preferred_element_type=F32)


def span(w):
    lo = lax.axis_index("band_lo")
    wave = lax.axis_index("band_hi") * (PAIR * WL) + (lo * WL + w) % (PAIR * WL)
    return (1024 * (16 + wave)).astype(F32)


def angle(n, m):
    inv = 1.0 / m
    q = jnp.floor(n * inv + 0.5)
    return turn((n - q * m) * inv)


def chirp_cols(level, first, lanes):
    x = (2 * (first + lax.broadcasted_iota(jnp.int32, (1, lanes), 1)) + 1).astype(F32)
    return turn(x * x * (level.astype(F32) * (0.5 / (N * N))))


def chirp_rows(level, row_pos):
    x = (2 * row_pos - (N - 1)).astype(F32)
    return turn(x * x * (level.astype(F32) * (0.5 / (N * N))))


def flip_matrix(flip, size):
    r = lax.broadcasted_iota(jnp.int32, (size, size), 0)
    c = lax.broadcasted_iota(jnp.int32, (size, size), 1)
    return jnp.where(jnp.where(flip, size - 1 - c, c) == r, 1.0, 0.0).astype(BF16)


def write_tables(tab, first, wave0):
    k = lax.broadcasted_iota(jnp.int32, (8, 128), 0) + 1
    lane = lax.broadcasted_iota(jnp.int32, (8, 128), 1)
    at, state = [], []
    for w in range(WL):
        m = span(wave0 + w)
        for t in range(0, CB, 128):
            x = 2 * (first + t + lane) + 1
            c, s = angle((x * k).astype(F32), m)
            rc, rs = angle((x * 8).astype(F32), m)
            at.append((w, t))
            state.append((c * NORM, s * NORM, rc, rs))
    for q in range(K // 16):
        for n, (w, t) in enumerate(at):
            c0, s0, rc, rs = state[n]
            c1, s1 = c0 * rc - s0 * rs, c0 * rs + s0 * rc
            rows, lanes = slice(16 * q, 16 * q + 16), slice(t, t + 128)
            tab[w, 0, rows, lanes] = jnp.concatenate([c0, c1], axis=0).astype(BF16)
            tab[w, 1, rows, lanes] = jnp.concatenate([s0, s1], axis=0).astype(BF16)
            state[n] = (c1 * rc - s1 * rs, c1 * rs + s1 * rc, rc, rs)


def forward_kernel(level, ph_r, ph_l, ap_r, ap_l, tab, tab2, fld, out, *scratch):
    n_sub = CB // SUB
    e_all, o_all = scratch[:n_sub], scratch[n_sub : 2 * n_sub]
    xacc, yacc, tmp = scratch[2 * n_sub :]
    i = pl.program_id(0)
    row = lax.axis_index("row")
    mine = lax.axis_index("band_lo") * PART

    @pl.when(i == 0)
    def _():
        xacc[...] = jnp.zeros_like(xacc)
        yacc[...] = jnp.zeros_like(yacc)

    write_tables(tab, i * CB, 0)
    write_tables(tab2, i * CB, WL)
    dx = [chirp_cols(level[w], i * CB, CB) for w in range(WL)]
    ones = jnp.full((16, SUB), NORM, BF16)
    for n in range(n_sub):
        h = n * SUB
        e_s, o_s = e_all[n], o_all[n]
        cols = slice(h, h + SUB)
        mirror = slice(CB - SUB - h, CB - h)
        for r0 in range(0, ROWS, CHUNK):
            sl = pl.ds(pl.multiple_of((mine + r0) % ROWS, CHUNK), CHUNK)
            fr_c, fr_s = field(ph_r[sl, cols], ap_r[sl, cols].astype(F32))
            fl_c, fl_s = field(lane_rev(ph_l[sl, mirror]), lane_rev(ap_l[sl, mirror]).astype(F32))
            if r0 < PART:
                keep = slice(r0, r0 + CHUNK)
                fld[0, keep, cols] = fr_c
                fld[1, keep, cols] = fr_s
                fld[2, keep, cols] = fl_c
                fld[3, keep, cols] = fl_s
            ec, es = fr_c + fl_c, fr_s + fl_s
            oc, os = fr_c - fl_c, fr_s - fl_s
            for w in range(WL):
                dc, ds = dx[w][0][:, cols], dx[w][1][:, cols]
                e_s[w, 0, sl, :] = (ec * dc - es * ds).astype(BF16)
                e_s[w, 1, sl, :] = (ec * ds + es * dc).astype(BF16)
                o_s[w, 0, sl, :] = (oc * dc - os * ds).astype(BF16)
                o_s[w, 1, sl, :] = (oc * ds + os * dc).astype(BF16)
        for w in range(WL):
            c = jnp.concatenate([tab[w, 0, :, cols], ones], axis=0)
            s = tab[w, 1, :, cols]
            for part in range(2):
                xacc[w, part] += nt(c, e_s[w, part])
                yacc[w, part] += nt(s, o_s[w, part])

    @pl.when(i == HALF // CB - 1)
    def _():
        j = flip_matrix(row < 8, ROWS)
        pos = row * ROWS + lax.broadcasted_iota(jnp.int32, (1, ROWS), 1)
        for w in range(WL):
            dc, ds = chirp_rows(level[w], pos)
            xr, xi = xacc[w, 0], xacc[w, 1]
            yr, yi = yacc[w, 0], yacc[w, 1]
            xr, xi = xr * dc - xi * ds, xr * ds + xi * dc
            yr, yi = yr * dc - yi * ds, yr * ds + yi * dc
            x0 = (xr[K : K + 1], xi[K : K + 1])
            xr, xi = xr[:K], xi[:K]
            plus = (xr + yi, xi - yr)
            minus = (xr - yi, xi + yr)
            for part in range(2):
                tmp[pl.ds(8, K), :] = plus[part]
                tmp[pl.ds(7, 1), :] = x0[part]
                p = nn(tmp[pl.ds(7, K), :].astype(BF16), j).astype(BF16)
                m = nn(minus[part].astype(BF16), j).astype(BF16)
                at = (w * 2 + part) * GRP
                for g in range(8):
                    out[8 + g, at : at + GRP, :] = p[g * GRP : (g + 1) * GRP]
                    out[7 - g, at : at + GRP, :] = m[g * GRP : (g + 1) * GRP]


def focal_kernel(x, tab, seen, out, obs):
    low = lax.axis_index("row") < 8
    for w in range(WL):
        for r in range(GRP):
            obs[w, pl.ds(jnp.where(low, GRP - 1 - r, r), 1), :] = seen[w, r : r + 1, :]
    last = lax.broadcasted_iota(jnp.int32, (GRP, K), 1) == K - 1
    for w in range(WL):
        at = w * 2 * GRP
        acc_c = jnp.zeros((2 * GRP, K), F32)
        acc_s = jnp.zeros((2 * GRP, K), F32)
        centre = jnp.zeros((2 * GRP, BLK), F32)
        for i in range(STEPS):
            r = x[8 + i, at : at + 2 * GRP, :].astype(F32)
            l = x[7 - i, at : at + 2 * GRP, :].astype(F32)
            e = r + l
            centre = centre + e
            cols = slice(i * BLK, (i + 1) * BLK)
            acc_c = acc_c + nt(e.astype(BF16), tab[w, 0, :, cols])
            acc_s = acc_s + nt((r - l).astype(BF16), tab[w, 1, :, cols])
        centre = jnp.sum(centre, axis=1, keepdims=True) * NORM
        cr, ci = acc_c[:GRP], acc_c[GRP:]
        sr, si = acc_s[:GRP], acc_s[GRP:]
        rest = pltpu.roll(obs[w, :, K:], K - 1, 1)
        weighted = []
        for side, (fr, fi) in enumerate(
            (
                (jnp.where(last, centre[:GRP], cr + si), jnp.where(last, centre[GRP:], ci - sr)),
                (cr - si, ci + sr),
            )
        ):
            misfit = fr * fr + fi * fi - (rest if side == 0 else lane_rev(obs[w, :, :K]))
            weighted.append(
                [(misfit * fr).astype(BF16).astype(F32), (misfit * fi).astype(BF16).astype(F32)]
            )
        (pr, pi), (mr, mi) = weighted
        centre = jnp.concatenate([pr[:, K - 1 :], pi[:, K - 1 :]], axis=0) * NORM
        p = jnp.concatenate([jnp.where(last, 0.0, pr), jnp.where(last, 0.0, pi)], axis=0)
        m = jnp.concatenate([mr, mi], axis=0)
        s = (p + m).astype(BF16)
        d = (p - m).astype(BF16)
        for i in range(STEPS):
            cols = slice(i * BLK, (i + 1) * BLK)
            bc = nn(s, tab[w, 0, :, cols]) + centre
            bs = nn(d, tab[w, 1, :, cols])
            bcr, bci, bsr, bsi = bc[:GRP], bc[GRP:], bs[:GRP], bs[GRP:]
            for block, re, im in ((8 + i, bcr - bsi, bci + bsr), (7 - i, bcr + bsi, bci - bsr)):
                re, im = re.astype(BF16), im.astype(BF16)
                for q in range(PAIR):
                    p = q if block >= 8 else PAIR - 1 - q
                    lanes = slice(p * PART, (p + 1) * PART)
                    out[q * 16 + block, at : at + GRP, :] = re[:, lanes]
                    out[q * 16 + block, at + GRP : at + 2 * GRP, :] = im[:, lanes]


def gradient_kernel(level, x, tab, tab2, fld, out, lhs, mid, sp, tmp):
    row = lax.axis_index("row")
    lo = lax.axis_index("band_lo")
    flip = row < 8
    j = flip_matrix(flip, PART)
    lane = lax.broadcasted_iota(jnp.int32, (1, PART), 1)
    pos = row * ROWS + lo * PART + jnp.where(flip, PART - 1 - lane, lane)
    for w in range(PAIR * WL):
        src = (lo + w // WL) % PAIR * 16
        dc, ds = chirp_rows(level[w], pos)
        p, m, b0 = [], [], []
        for part in range(2):
            at = (w % WL * 2 + part) * GRP
            for g in range(8):
                tmp[g * GRP : (g + 1) * GRP, :] = x[src + 8 + g, at : at + GRP, :].astype(F32)
            tmp[K : K + 8, :] = jnp.zeros((8, PART), F32)
            b0.append(tmp[0:1, :])
            p.append(tmp[pl.ds(1, K), :])
            m.append(
                jnp.concatenate([x[src + 7 - g, at : at + GRP, :] for g in range(8)], axis=0).astype(F32)
            )
        for n, (re, im) in enumerate(
            ((p[0] + m[0], p[1] + m[1]), (p[0] - m[0], p[1] - m[1]))
        ):
            lhs[w, n, :PART] = nt(j, (re * dc + im * ds).astype(BF16)).astype(BF16)
            lhs[w, n, PART:] = nt(j, (im * dc - re * ds).astype(BF16)).astype(BF16)
        for part, v in enumerate((b0[0] * dc + b0[1] * ds, b0[1] * dc - b0[0] * ds)):
            v = jnp.broadcast_to((v * NORM).astype(BF16), (128, PART))
            mid[w, part] = nt(j, v)

    def block(i, _):
        base = pl.multiple_of(i * CB, CB)
        dx = [chirp_cols(level[w], base, CB) for w in range(PAIR * WL)]
        per = M // CB
        right = 4 + i // per, pl.multiple_of(i % per * CB, CB)
        left = 3 - i // per, pl.multiple_of((per - 1 - i % per) * CB, CB)
        for h in range(0, CB, SUB):
            cols = pl.ds(pl.multiple_of(base + h, SUB), SUB)
            for w in range(PAIR * WL):
                table = tab if w < WL else tab2
                for n in range(2):
                    sp[w, n, :, h : h + SUB] = nn(lhs[w, n], table[w % WL, n, :, cols])
            for r0 in range(0, PART, CHUNK):
                sl = slice(r0, r0 + CHUNK)
                im = slice(PART + r0, PART + r0 + CHUNK)
                tot = [0.0, 0.0, 0.0, 0.0]
                for w in range(PAIR * WL):
                    dc, ds = dx[w][0][:, h : h + SUB], dx[w][1][:, h : h + SUB]
                    m = [
                        jnp.concatenate([mid[w, part, sl, :]] * (SUB // 128), axis=1)
                        for part in range(2)
                    ]
                    cr, ci = sp[w, 0, sl, h : h + SUB] + m[0], sp[w, 0, im, h : h + SUB] + m[1]
                    sr, si = sp[w, 1, sl, h : h + SUB], sp[w, 1, im, h : h + SUB]
                    tot[0] += cr * dc + ci * ds
                    tot[1] += ci * dc - cr * ds
                    tot[2] += sr * dc + si * ds
                    tot[3] += si * dc - sr * ds
                cr, ci, sr, si = tot
                g_r = (ci + sr) * fld[0, sl, cols] - (cr - si) * fld[1, sl, cols]
                g_l = (ci - sr) * fld[2, sl, cols] - (cr + si) * fld[3, sl, cols]
                out[right[0], sl, pl.ds(right[1] + h, SUB)] = g_r.astype(BF16)
                out[left[0], sl, pl.ds(left[1] + (CB - SUB - h), SUB)] = lane_rev(g_l).astype(BF16)
        return 0

    lax.fori_loop(0, HALF // CB, block, 0)


def run_forward(level, phase, aperture):
    smem = pl.BlockSpec(memory_space=pltpu.SMEM)
    right = pl.BlockSpec((ROWS, CB), lambda i: (0, HALF // CB + i))
    left = pl.BlockSpec((ROWS, CB), lambda i: (0, HALF // CB - 1 - i))
    return pl.pallas_call(
        forward_kernel,
        grid=(HALF // CB,),
        out_shape=(
            jax.ShapeDtypeStruct((WL, 2, K, HALF), BF16),
            jax.ShapeDtypeStruct((WL, 2, K, HALF), BF16),
            jax.ShapeDtypeStruct((4, PART, HALF), F32),
            jax.ShapeDtypeStruct((16, WL * 2 * GRP, ROWS), BF16),
        ),
        in_specs=[smem, right, left, right, left],
        out_specs=(
            pl.BlockSpec((WL, 2, K, CB), lambda i: (0, 0, 0, i)),
            pl.BlockSpec((WL, 2, K, CB), lambda i: (0, 0, 0, i)),
            pl.BlockSpec((4, PART, CB), lambda i: (0, 0, i)),
            pl.BlockSpec((16, WL * 2 * GRP, ROWS), lambda i: (0, 0, 0)),
        ),
        scratch_shapes=[pltpu.VMEM((WL, 2, ROWS, SUB), BF16)] * (2 * CB // SUB)
        + [
            pltpu.VMEM((WL, 2, K + 16, ROWS), F32),
            pltpu.VMEM((WL, 2, K, ROWS), F32),
            pltpu.VMEM((K + 16, ROWS), F32),
        ],
        compiler_params=pltpu.CompilerParams(vmem_limit_bytes=60 * 2**20),
        name="forward",
    )(level, phase, phase, aperture, aperture)


def run_focal(x, tab, seen):
    return pl.pallas_call(
        focal_kernel,
        out_shape=jax.ShapeDtypeStruct((PAIR * 16, WL * 2 * GRP, PART), BF16),
        in_specs=[pl.BlockSpec(memory_space=pltpu.VMEM)] * 3,
        out_specs=pl.BlockSpec(memory_space=pltpu.VMEM),
        scratch_shapes=[pltpu.VMEM((WL, GRP, M), F32)],
        compiler_params=pltpu.CompilerParams(vmem_limit_bytes=20 * 2**20),
        cost_estimate=pl.CostEstimate(flops=2**34, bytes_accessed=2**26, transcendentals=0),
        name="focal",
    )(x, tab, seen)


def run_gradient(level, x, tab, tab2, fld):
    return pl.pallas_call(
        gradient_kernel,
        out_shape=jax.ShapeDtypeStruct((8, PART, M), BF16),
        in_specs=[pl.BlockSpec(memory_space=pltpu.SMEM)] + [pl.BlockSpec(memory_space=pltpu.VMEM)] * 4,
        out_specs=pl.BlockSpec(memory_space=pltpu.VMEM),
        scratch_shapes=[
            pltpu.VMEM((PAIR * WL, 2, 2 * PART, K), BF16),
            pltpu.VMEM((PAIR * WL, 2, PART, 128), F32),
            pltpu.VMEM((PAIR * WL, 2, 2 * PART, CB), F32),
            pltpu.VMEM((K + 8, PART), F32),
        ],
        compiler_params=pltpu.CompilerParams(vmem_limit_bytes=28 * 2**20),
        cost_estimate=pl.CostEstimate(flops=2**34, bytes_accessed=2**26, transcendentals=0),
        name="gradient",
    )(level, x, tab, tab2, fld)


def local(phase, aperture, defocus_index, intensity):
    level = defocus_index.astype(jnp.int32)
    levels = jnp.concatenate([level, lax.ppermute(level, "band_lo", [(0, 1), (1, 0)])])
    tab, tab2, fld, sent = run_forward(level, phase, aperture)
    sent, levels = lax.optimization_barrier((sent, levels))
    got = lax.all_to_all(sent, "row", 0, 0, tiled=True)
    sent = run_focal(got, tab, intensity)
    got = lax.all_to_all(sent, ("band_lo", "row"), 0, 0, tiled=True)
    parts = run_gradient(levels, got, tab, tab2, fld)
    parts = lax.all_to_all(parts, ("band_hi", "band_lo"), 0, 0, tiled=True)
    return jnp.sum(parts.reshape(8 // PAIR, ROWS, M).astype(F32), axis=0)


def solution(mesh):
    band, row = mesh.devices.shape
    split = Mesh(mesh.devices.reshape(band // PAIR, PAIR, row), ("band_hi", "band_lo", "row"))
    both = ("band_hi", "band_lo")
    return jax.shard_map(
        local,
        mesh=split,
        in_specs=(P("row", None), P("row", None), P(both), P(both, "row", None)),
        out_specs=P("row", both),
        check_vma=False,
    )
```

```python
import math

import jax
import jax.numpy as jnp
from jax import lax
from jax.experimental import pallas as pl
from jax.experimental.pallas import tpu as pltpu
from jax.sharding import Mesh
from jax.sharding import PartitionSpec as P

F32 = jnp.float32
BF16 = jnp.bfloat16
N = 4096
M = 512
HALF = N // 2
K = M // 2
ROWS = 256
BLK = 256
CB = 512
SUB = 256
FWD_VMEM = 57
SIDE_VMEM = 57
STEP = 256
DOT = 512
CHUNK = 32
STEPS = HALF // BLK
WL = 2
GRP = 32
PAIR = 2
PART = ROWS // PAIR
NORM = 1.0 / math.sqrt(N)

SIN_C = (9.99999246e-01, -1.66656827e-01, 8.31325871e-03, -1.85243573e-04)
COS_C = (9.99999953e-01, -4.99999053e-01, 4.16635847e-02, -1.38537043e-03, 2.31539316e-05)
SIN_T = (6.28318492, -41.34159016, 81.5999729, -76.61480386, 41.34439753, -12.47366849)
COS_T = (0.99999999, -19.73920453, 64.93911898, -85.45016555, 60.16783172, -25.96831326, 6.52961036)


def poly(coefs, y):
    acc = coefs[-1]
    for c in coefs[-2::-1]:
        acc = acc * y + c
    return acc


def turn(t):
    t = t - jnp.floor(t + 0.5)
    y = t * t
    return poly(COS_T, y), t * poly(SIN_T, y)


def unit(phi):
    y = phi * phi
    r2 = math.sqrt(2.0)
    c = poly([r2 * v / 4.0**n for n, v in enumerate(COS_C)], y)
    s = phi * poly([0.5 * r2 * v / 4.0**n for n, v in enumerate(SIN_C)], y)
    return c, s


def field(phi, amp):
    c, s = unit(phi)
    a_s = amp * s
    return amp - s * a_s, a_s * c


def lane_rev(x):
    rows, lanes = x.shape
    idx = 127 - lax.broadcasted_iota(jnp.int32, (rows, 128), 1)
    parts = [
        jnp.take_along_axis(x[:, s : s + 128], idx, axis=1, mode="promise_in_bounds")
        for s in range(lanes - 128, -1, -128)
    ]
    return jnp.concatenate(parts, axis=1) if len(parts) > 1 else parts[0]


def nt(a, b):
    return lax.dot_general(a, b, (((1,), (1,)), ((), ())), preferred_element_type=F32)


def nn(a, b):
    return lax.dot_general(a, b, (((1,), (0,)), ((), ())), preferred_element_type=F32)


def span(w):
    lo = lax.axis_index("band_lo")
    wave = lax.axis_index("band_hi") * (PAIR * WL) + (lo * WL + w) % (PAIR * WL)
    return (1024 * (16 + wave)).astype(F32)


def angle(n, m):
    inv = 1.0 / m
    q = jnp.floor(n * inv + 0.5)
    return turn((n - q * m) * inv)


def chirp_cols(level, first, lanes):
    x = (2 * (first + lax.broadcasted_iota(jnp.int32, (1, lanes), 1)) + 1).astype(F32)
    return turn(x * x * (level.astype(F32) * (0.5 / (N * N))))


def chirp_rows(level, row_pos):
    x = (2 * row_pos - (N - 1)).astype(F32)
    return turn(x * x * (level.astype(F32) * (0.5 / (N * N))))


def flip_matrix(flip, size):
    r = lax.broadcasted_iota(jnp.int32, (size, size), 0)
    c = lax.broadcasted_iota(jnp.int32, (size, size), 1)
    return jnp.where(jnp.where(flip, size - 1 - c, c) == r, 1.0, 0.0).astype(BF16)


def write_tables(tab, first, wave0, place):
    k = lax.broadcasted_iota(jnp.int32, (8, 128), 0) + 1
    lane = lax.broadcasted_iota(jnp.int32, (8, 128), 1)
    at, state = [], []
    for w in range(WL):
        m = span(wave0 + w)
        for t in range(0, CB, 128):
            x = 2 * (first + t + lane) + 1
            c, s = angle((x * k).astype(F32), m)
            rc, rs = angle((x * 8).astype(F32), m)
            at.append((w, pl.ds(pl.multiple_of(place + t, 128), 128)))
            state.append((c * NORM, s * NORM, rc, rs))
    for q in range(K // 16):
        rows = slice(16 * q, 16 * q + 16)
        for n, (w, lanes) in enumerate(at):
            c0, s0, rc, rs = state[n]
            c1, s1 = c0 * rc - s0 * rs, c0 * rs + s0 * rc
            tab[w, 0, rows, lanes] = jnp.concatenate([c0, c1], axis=0).astype(BF16)
            tab[w, 1, rows, lanes] = jnp.concatenate([s0, s1], axis=0).astype(BF16)
            state[n] = (c1 * rc - s1 * rs, c1 * rs + s1 * rc, rc, rs)


def forward_kernel(level, ph_in, ap_in, out, *scratch):
    e_s, o_s, ph, ap, tab, xacc, yacc, tmp, sem_in = scratch
    row = lax.axis_index("row")
    blocks = HALF // CB

    def right(i):
        return pl.ds(pl.multiple_of(HALF + i * CB, CB), CB)

    def left(i):
        return pl.ds(pl.multiple_of(HALF - CB - i * CB, CB), CB)

    def fetch(i):
        return [
            pltpu.make_async_copy(src.at[:, cols], dst.at[:, cols], sem_in.at[i, n])
            for n, (src, dst, cols) in enumerate(
                ((ph_in, ph, right(i)), (ph_in, ph, left(i)), (ap_in, ap, right(i)), (ap_in, ap, left(i)))
            )
        ]

    for i in range(blocks):
        for copy in fetch(i):
            copy.start()
    ones = jnp.full((16, HALF), NORM, BF16)

    def block(i, _):
        base = pl.multiple_of(i * CB, CB)
        cols = pl.ds(base, CB)

        def tables(n, _):
            write_tables(tab, base, 0, base)
            return 0

        lax.fori_loop(0, jnp.minimum(i + 1, 1), tables, 0)
        for copy in fetch(i):
            copy.wait()
        dx = [chirp_cols(level[w], base, CB) for w in range(WL)]

        def rows(t, _):
            for r1 in range(0, STEP, CHUNK):
                for h in range(0, CB, SUB):
                    sl = pl.ds(pl.multiple_of(t * STEP + r1, CHUNK), CHUNK)
                    here = slice(h, h + SUB)
                    there = pl.ds(pl.multiple_of(base + h, SUB), SUB)
                    straight = pl.ds(pl.multiple_of(HALF + base + h, SUB), SUB)
                    mirror = pl.ds(pl.multiple_of(HALF - SUB - base - h, SUB), SUB)
                    fr_c, fr_s = field(ph[sl, straight], ap[sl, straight].astype(F32))
                    fl_c, fl_s = field(lane_rev(ph[sl, mirror]), lane_rev(ap[sl, mirror]).astype(F32))
                    ec, es = fr_c + fl_c, fr_s + fl_s
                    oc, os = fr_c - fl_c, fr_s - fl_s
                    for w in range(WL):
                        dc, ds = dx[w][0][:, here], dx[w][1][:, here]
                        e_s[w, 0, sl, there] = (ec * dc - es * ds).astype(BF16)
                        e_s[w, 1, sl, there] = (ec * ds + es * dc).astype(BF16)
                        o_s[w, 0, sl, there] = (oc * dc - os * ds).astype(BF16)
                        o_s[w, 1, sl, there] = (oc * ds + os * dc).astype(BF16)
            return 0

        lax.fori_loop(0, ROWS // STEP, rows, 0)

        return 0

    lax.fori_loop(0, blocks, block, 0)
    def dots(w, _):
        c = jnp.concatenate([tab[w, 0], ones], axis=0)
        s = tab[w, 1]
        for part in range(2):
            xacc[w, part] = nt(c, e_s[w, part])
            yacc[w, part] = nt(s, o_s[w, part])
        return 0

    lax.fori_loop(0, WL, dots, 0)
    j = flip_matrix(row < 8, ROWS)
    pos = row * ROWS + lax.broadcasted_iota(jnp.int32, (1, ROWS), 1)
    for w in range(WL):
        dc, ds = chirp_rows(level[w], pos)
        xr, xi = xacc[w, 0], xacc[w, 1]
        yr, yi = yacc[w, 0], yacc[w, 1]
        xr, xi = xr * dc - xi * ds, xr * ds + xi * dc
        yr, yi = yr * dc - yi * ds, yr * ds + yi * dc
        x0 = (xr[K : K + 1], xi[K : K + 1])
        xr, xi = xr[:K], xi[:K]
        plus = (xr + yi, xi - yr)
        minus = (xr - yi, xi + yr)
        for part in range(2):
            tmp[pl.ds(8, K), :] = plus[part]
            tmp[pl.ds(7, 1), :] = x0[part]
            p = nn(tmp[pl.ds(7, K), :].astype(BF16), j).astype(BF16)
            m = nn(minus[part].astype(BF16), j).astype(BF16)
            at = (w * 2 + part) * GRP
            for g in range(8):
                out[8 + g, at : at + GRP, :] = p[g * GRP : (g + 1) * GRP]
                out[7 - g, at : at + GRP, :] = m[g * GRP : (g + 1) * GRP]


def side_kernel(ph_r, ph_l, ap_r, ap_l, tab, tab2, fld):
    i = pl.program_id(0)
    write_tables(tab, i * CB, 0, 0)
    write_tables(tab2, i * CB, WL, 0)

    def rows(t, _):
        sl = pl.ds(pl.multiple_of(t * CHUNK, CHUNK), CHUNK)
        fld[0, sl, :], fld[1, sl, :] = field(ph_r[sl, :], ap_r[sl, :].astype(F32))
        fld[2, sl, :], fld[3, sl, :] = field(lane_rev(ph_l[sl, :]), lane_rev(ap_l[sl, :]).astype(F32))
        return 0

    lax.fori_loop(0, PART // CHUNK, rows, 0)


def focal_kernel(x, tab, seen, out, obs):
    low = lax.axis_index("row") < 8
    for w in range(WL):
        for r in range(GRP):
            obs[w, pl.ds(jnp.where(low, GRP - 1 - r, r), 1), :] = seen[w, r : r + 1, :]
    last = lax.broadcasted_iota(jnp.int32, (GRP, K), 1) == K - 1
    for w in range(WL):
        at = w * 2 * GRP
        acc_c = jnp.zeros((2 * GRP, K), F32)
        acc_s = jnp.zeros((2 * GRP, K), F32)
        centre = jnp.zeros((2 * GRP, BLK), F32)
        for i in range(STEPS):
            r = x[8 + i, at : at + 2 * GRP, :].astype(F32)
            l = x[7 - i, at : at + 2 * GRP, :].astype(F32)
            e = r + l
            centre = centre + e
            cols = slice(i * BLK, (i + 1) * BLK)
            acc_c = acc_c + nt(e.astype(BF16), tab[w, 0, :, cols])
            acc_s = acc_s + nt((r - l).astype(BF16), tab[w, 1, :, cols])
        centre = jnp.sum(centre, axis=1, keepdims=True) * NORM
        cr, ci = acc_c[:GRP], acc_c[GRP:]
        sr, si = acc_s[:GRP], acc_s[GRP:]
        rest = pltpu.roll(obs[w, :, K:], K - 1, 1)
        weighted = []
        for side, (fr, fi) in enumerate(
            (
                (jnp.where(last, centre[:GRP], cr + si), jnp.where(last, centre[GRP:], ci - sr)),
                (cr - si, ci + sr),
            )
        ):
            misfit = fr * fr + fi * fi - (rest if side == 0 else lane_rev(obs[w, :, :K]))
            weighted.append(
                [(misfit * fr).astype(BF16).astype(F32), (misfit * fi).astype(BF16).astype(F32)]
            )
        (pr, pi), (mr, mi) = weighted
        centre = jnp.concatenate([pr[:, K - 1 :], pi[:, K - 1 :]], axis=0) * NORM
        p = jnp.concatenate([jnp.where(last, 0.0, pr), jnp.where(last, 0.0, pi)], axis=0)
        m = jnp.concatenate([mr, mi], axis=0)
        s = (p + m).astype(BF16)
        d = (p - m).astype(BF16)
        for i in range(STEPS):
            cols = slice(i * BLK, (i + 1) * BLK)
            bc = nn(s, tab[w, 0, :, cols]) + centre
            bs = nn(d, tab[w, 1, :, cols])
            bcr, bci, bsr, bsi = bc[:GRP], bc[GRP:], bs[:GRP], bs[GRP:]
            for block, re, im in ((8 + i, bcr - bsi, bci + bsr), (7 - i, bcr + bsi, bci - bsr)):
                re, im = re.astype(BF16), im.astype(BF16)
                for q in range(PAIR):
                    p = q if block >= 8 else PAIR - 1 - q
                    lanes = slice(p * PART, (p + 1) * PART)
                    out[q * 16 + block, at : at + GRP, :] = re[:, lanes]
                    out[q * 16 + block, at + GRP : at + 2 * GRP, :] = im[:, lanes]


def gradient_kernel(level, x, tab, tab2, fld, out, lhs, mid, sp, tmp):
    row = lax.axis_index("row")
    lo = lax.axis_index("band_lo")
    flip = row < 8
    j = flip_matrix(flip, PART)
    lane = lax.broadcasted_iota(jnp.int32, (1, PART), 1)
    pos = row * ROWS + lo * PART + jnp.where(flip, PART - 1 - lane, lane)
    for w in range(PAIR * WL):
        src = (lo + w // WL) % PAIR * 16
        dc, ds = chirp_rows(level[w], pos)
        p, m, b0 = [], [], []
        for part in range(2):
            at = (w % WL * 2 + part) * GRP
            for g in range(8):
                tmp[g * GRP : (g + 1) * GRP, :] = x[src + 8 + g, at : at + GRP, :].astype(F32)
            tmp[K : K + 8, :] = jnp.zeros((8, PART), F32)
            b0.append(tmp[0:1, :])
            p.append(tmp[pl.ds(1, K), :])
            m.append(
                jnp.concatenate([x[src + 7 - g, at : at + GRP, :] for g in range(8)], axis=0).astype(F32)
            )
        for n, (re, im) in enumerate(
            ((p[0] + m[0], p[1] + m[1]), (p[0] - m[0], p[1] - m[1]))
        ):
            lhs[w, n, :PART] = nt(j, (re * dc + im * ds).astype(BF16)).astype(BF16)
            lhs[w, n, PART:] = nt(j, (im * dc - re * ds).astype(BF16)).astype(BF16)
        for part, v in enumerate((b0[0] * dc + b0[1] * ds, b0[1] * dc - b0[0] * ds)):
            v = jnp.broadcast_to((v * NORM).astype(BF16), (128, PART))
            mid[w, part] = nt(j, v)

    def block(i, _):
        base = pl.multiple_of(i * CB, CB)
        dx = [chirp_cols(level[w], base, CB) for w in range(PAIR * WL)]
        per = M // CB
        right = 4 + i // per, pl.multiple_of(i % per * CB, CB)
        left = 3 - i // per, pl.multiple_of((per - 1 - i % per) * CB, CB)
        for h in range(0, CB, SUB):
            cols = pl.ds(pl.multiple_of(base + h, SUB), SUB)
            for w in range(PAIR * WL):
                table = tab if w < WL else tab2
                for n in range(2):
                    sp[w, n, :, h : h + SUB] = nn(lhs[w, n], table[w % WL, n, :, cols])
            for r0 in range(0, PART, CHUNK):
                sl = slice(r0, r0 + CHUNK)
                im = slice(PART + r0, PART + r0 + CHUNK)
                tot = [0.0, 0.0, 0.0, 0.0]
                for w in range(PAIR * WL):
                    dc, ds = dx[w][0][:, h : h + SUB], dx[w][1][:, h : h + SUB]
                    m = [
                        jnp.concatenate([mid[w, part, sl, :]] * (SUB // 128), axis=1)
                        for part in range(2)
                    ]
                    cr, ci = sp[w, 0, sl, h : h + SUB] + m[0], sp[w, 0, im, h : h + SUB] + m[1]
                    sr, si = sp[w, 1, sl, h : h + SUB], sp[w, 1, im, h : h + SUB]
                    tot[0] += cr * dc + ci * ds
                    tot[1] += ci * dc - cr * ds
                    tot[2] += sr * dc + si * ds
                    tot[3] += si * dc - sr * ds
                cr, ci, sr, si = tot
                g_r = (ci + sr) * fld[0, sl, cols] - (cr - si) * fld[1, sl, cols]
                g_l = (ci - sr) * fld[2, sl, cols] - (cr + si) * fld[3, sl, cols]
                out[right[0], sl, pl.ds(right[1] + h, SUB)] = g_r.astype(BF16)
                out[left[0], sl, pl.ds(left[1] + (CB - SUB - h), SUB)] = lane_rev(g_l).astype(BF16)
        return 0

    lax.fori_loop(0, HALF // CB, block, 0)


def run_forward(level, phase, aperture):
    any_space = pl.BlockSpec(memory_space=pl.ANY)
    return pl.pallas_call(
        forward_kernel,
        out_shape=jax.ShapeDtypeStruct((16, WL * 2 * GRP, ROWS), BF16),
        in_specs=[pl.BlockSpec(memory_space=pltpu.SMEM), any_space, any_space],
        out_specs=pl.BlockSpec(memory_space=pltpu.VMEM),
        scratch_shapes=[pltpu.VMEM((WL, 2, ROWS, HALF), BF16)] * 2
        + [
            pltpu.VMEM((ROWS, N), F32),
            pltpu.VMEM((ROWS, N), jnp.int32),
            pltpu.VMEM((WL, 2, K, HALF), BF16),
            pltpu.VMEM((WL, 2, K + 16, ROWS), F32),
            pltpu.VMEM((WL, 2, K, ROWS), F32),
            pltpu.VMEM((K + 16, ROWS), F32),
            pltpu.SemaphoreType.DMA((HALF // CB, 4)),
        ],
        compiler_params=pltpu.CompilerParams(vmem_limit_bytes=FWD_VMEM * 2**20),
        name="forward",
    )(level, phase, aperture)


def run_side(phase, aperture):
    right = pl.BlockSpec((PART, CB), lambda i: (0, HALF // CB + i))
    left = pl.BlockSpec((PART, CB), lambda i: (0, HALF // CB - 1 - i))
    return pl.pallas_call(
        side_kernel,
        grid=(HALF // CB,),
        out_shape=(
            jax.ShapeDtypeStruct((WL, 2, K, HALF), BF16),
            jax.ShapeDtypeStruct((WL, 2, K, HALF), BF16),
            jax.ShapeDtypeStruct((4, PART, HALF), F32),
        ),
        in_specs=[right, left, right, left],
        out_specs=(
            pl.BlockSpec((WL, 2, K, CB), lambda i: (0, 0, 0, i)),
            pl.BlockSpec((WL, 2, K, CB), lambda i: (0, 0, 0, i)),
            pl.BlockSpec((4, PART, CB), lambda i: (0, 0, i)),
        ),
        compiler_params=pltpu.CompilerParams(vmem_limit_bytes=SIDE_VMEM * 2**20),
        cost_estimate=pl.CostEstimate(flops=2**32, bytes_accessed=2**24, transcendentals=0),
        name="side",
    )(phase, phase, aperture, aperture)


def run_focal(x, tab, seen):
    return pl.pallas_call(
        focal_kernel,
        out_shape=jax.ShapeDtypeStruct((PAIR * 16, WL * 2 * GRP, PART), BF16),
        in_specs=[pl.BlockSpec(memory_space=pltpu.VMEM)] * 3,
        out_specs=pl.BlockSpec(memory_space=pltpu.VMEM),
        scratch_shapes=[pltpu.VMEM((WL, GRP, M), F32)],
        compiler_params=pltpu.CompilerParams(vmem_limit_bytes=20 * 2**20),
        cost_estimate=pl.CostEstimate(flops=2**34, bytes_accessed=2**26, transcendentals=0),
        name="focal",
    )(x, tab, seen)


def run_gradient(level, x, tab, tab2, fld):
    return pl.pallas_call(
        gradient_kernel,
        out_shape=jax.ShapeDtypeStruct((8, PART, M), BF16),
        in_specs=[pl.BlockSpec(memory_space=pltpu.SMEM)] + [pl.BlockSpec(memory_space=pltpu.VMEM)] * 4,
        out_specs=pl.BlockSpec(memory_space=pltpu.VMEM),
        scratch_shapes=[
            pltpu.VMEM((PAIR * WL, 2, 2 * PART, K), BF16),
            pltpu.VMEM((PAIR * WL, 2, PART, 128), F32),
            pltpu.VMEM((PAIR * WL, 2, 2 * PART, CB), F32),
            pltpu.VMEM((K + 8, PART), F32),
        ],
        compiler_params=pltpu.CompilerParams(vmem_limit_bytes=28 * 2**20),
        cost_estimate=pl.CostEstimate(flops=2**34, bytes_accessed=2**26, transcendentals=0),
        name="gradient",
    )(level, x, tab, tab2, fld)


def local(phase, aperture, defocus_index, intensity):
    level = defocus_index.astype(jnp.int32)
    levels = jnp.concatenate([level, lax.ppermute(level, "band_lo", [(0, 1), (1, 0)])])
    sent = run_forward(level, phase, aperture)
    sent, levels, phase, aperture = lax.optimization_barrier((sent, levels, phase, aperture))
    got = lax.all_to_all(sent, "row", 0, 0, tiled=True)
    mine = lax.axis_index("band_lo") * PART
    tab, tab2, fld = run_side(
        lax.dynamic_slice_in_dim(phase, mine, PART, 0), lax.dynamic_slice_in_dim(aperture, mine, PART, 0)
    )
    got, tab, tab2, fld = lax.optimization_barrier((got, tab, tab2, fld))
    sent = run_focal(got, tab, intensity)
    got = lax.all_to_all(sent, ("band_lo", "row"), 0, 0, tiled=True)
    parts = run_gradient(levels, got, tab, tab2, fld)
    parts = lax.all_to_all(parts, ("band_hi", "band_lo"), 0, 0, tiled=True)
    return jnp.sum(parts.reshape(8 // PAIR, ROWS, M).astype(F32), axis=0)


def solution(mesh):
    band, row = mesh.devices.shape
    split = Mesh(mesh.devices.reshape(band // PAIR, PAIR, row), ("band_hi", "band_lo", "row"))
    both = ("band_hi", "band_lo")
    return jax.shard_map(
        local,
        mesh=split,
        in_specs=(P("row", None), P("row", None), P(both), P(both, "row", None)),
        out_specs=P("row", both),
        check_vma=False,
    )
```

```python
import math

import jax
import jax.numpy as jnp
from jax import lax
from jax.experimental import pallas as pl
from jax.experimental.pallas import tpu as pltpu
from jax.sharding import Mesh
from jax.sharding import PartitionSpec as P

F32 = jnp.float32
BF16 = jnp.bfloat16
N = 4096
M = 512
HALF = N // 2
K = M // 2
ROWS = 256
BLK = 256
CB = 512
SUB = 256
FWD_VMEM = 57
SIDE_VMEM = 57
FAR = 8
STEP = 256
DOT = 512
CHUNK = 32
STEPS = HALF // BLK
WL = 2
GRP = 32
PAIR = 2
PART = ROWS // PAIR
NORM = 1.0 / math.sqrt(N)

SIN_C = (9.99999246e-01, -1.66656827e-01, 8.31325871e-03, -1.85243573e-04)
COS_C = (9.99999953e-01, -4.99999053e-01, 4.16635847e-02, -1.38537043e-03, 2.31539316e-05)
SIN_T = (6.28318492, -41.34159016, 81.5999729, -76.61480386, 41.34439753, -12.47366849)
COS_T = (0.99999999, -19.73920453, 64.93911898, -85.45016555, 60.16783172, -25.96831326, 6.52961036)


def poly(coefs, y):
    acc = coefs[-1]
    for c in coefs[-2::-1]:
        acc = acc * y + c
    return acc


def turn(t):
    t = t - jnp.floor(t + 0.5)
    y = t * t
    return poly(COS_T, y), t * poly(SIN_T, y)


def unit(phi):
    y = phi * phi
    r2 = math.sqrt(2.0)
    c = poly([r2 * v / 4.0**n for n, v in enumerate(COS_C)], y)
    s = phi * poly([0.5 * r2 * v / 4.0**n for n, v in enumerate(SIN_C)], y)
    return c, s


def field(phi, amp):
    c, s = unit(phi)
    a_s = amp * s
    return amp - s * a_s, a_s * c


def lane_rev(x):
    rows, lanes = x.shape
    idx = 127 - lax.broadcasted_iota(jnp.int32, (rows, 128), 1)
    parts = [
        jnp.take_along_axis(x[:, s : s + 128], idx, axis=1, mode="promise_in_bounds")
        for s in range(lanes - 128, -1, -128)
    ]
    return jnp.concatenate(parts, axis=1) if len(parts) > 1 else parts[0]


def nt(a, b):
    return lax.dot_general(a, b, (((1,), (1,)), ((), ())), preferred_element_type=F32)


def nn(a, b):
    return lax.dot_general(a, b, (((1,), (0,)), ((), ())), preferred_element_type=F32)


def span(w):
    lo = lax.axis_index("band_lo")
    wave = lax.axis_index("band_hi") * (PAIR * WL) + (lo * WL + w) % (PAIR * WL)
    return (1024 * (16 + wave)).astype(F32)


def angle(n, m):
    inv = 1.0 / m
    q = jnp.floor(n * inv + 0.5)
    return turn((n - q * m) * inv)


def chirp_cols(level, first, lanes):
    x = (2 * (first + lax.broadcasted_iota(jnp.int32, (1, lanes), 1)) + 1).astype(F32)
    return turn(x * x * (level.astype(F32) * (0.5 / (N * N))))


def chirp_rows(level, row_pos):
    x = (2 * row_pos - (N - 1)).astype(F32)
    return turn(x * x * (level.astype(F32) * (0.5 / (N * N))))


def flip_matrix(flip, size):
    r = lax.broadcasted_iota(jnp.int32, (size, size), 0)
    c = lax.broadcasted_iota(jnp.int32, (size, size), 1)
    return jnp.where(jnp.where(flip, size - 1 - c, c) == r, 1.0, 0.0).astype(BF16)


def write_tables(tab, first, wave0, place):
    k = lax.broadcasted_iota(jnp.int32, (8, 128), 0) + 1
    lane = lax.broadcasted_iota(jnp.int32, (8, 128), 1)
    at, state = [], []
    for w in range(WL):
        m = span(wave0 + w)
        for t in range(0, CB, 128):
            x = 2 * (first + t + lane) + 1
            c, s = angle((x * k).astype(F32), m)
            rc, rs = angle((x * 8).astype(F32), m)
            at.append((w, pl.ds(pl.multiple_of(place + t, 128), 128)))
            state.append((c * NORM, s * NORM, rc, rs))
    for q in range(K // 16):
        rows = slice(16 * q, 16 * q + 16)
        for n, (w, lanes) in enumerate(at):
            c0, s0, rc, rs = state[n]
            c1, s1 = c0 * rc - s0 * rs, c0 * rs + s0 * rc
            tab[w, 0, rows, lanes] = jnp.concatenate([c0, c1], axis=0).astype(BF16)
            tab[w, 1, rows, lanes] = jnp.concatenate([s0, s1], axis=0).astype(BF16)
            state[n] = (c1 * rc - s1 * rs, c1 * rs + s1 * rc, rc, rs)


def forward_kernel(level, ph_in, ap_in, out, *scratch):
    e_s, o_s, ph, ap, tab, xacc, yacc, tmp, sem_in = scratch
    row = lax.axis_index("row")
    blocks = HALF // CB

    def right(i):
        return pl.ds(pl.multiple_of(HALF + i * CB, CB), CB)

    def left(i):
        return pl.ds(pl.multiple_of(HALF - CB - i * CB, CB), CB)

    def fetch(i):
        return [
            pltpu.make_async_copy(src.at[:, cols], dst.at[:, cols], sem_in.at[i, n])
            for n, (src, dst, cols) in enumerate(
                ((ph_in, ph, right(i)), (ph_in, ph, left(i)), (ap_in, ap, right(i)), (ap_in, ap, left(i)))
            )
        ]

    for i in range(blocks):
        for copy in fetch(i):
            copy.start()
    ones = jnp.full((16, HALF), NORM, BF16)

    def block(i, _):
        base = pl.multiple_of(i * CB, CB)
        cols = pl.ds(base, CB)

        def tables(n, _):
            write_tables(tab, base, 0, base)
            return 0

        lax.fori_loop(0, jnp.minimum(i + 1, 1), tables, 0)
        for copy in fetch(i):
            copy.wait()
        dx = [chirp_cols(level[w], base, CB) for w in range(WL)]

        def rows(t, _):
            for r1 in range(0, STEP, CHUNK):
                for h in range(0, CB, SUB):
                    sl = pl.ds(pl.multiple_of(t * STEP + r1, CHUNK), CHUNK)
                    here = slice(h, h + SUB)
                    there = pl.ds(pl.multiple_of(base + h, SUB), SUB)
                    straight = pl.ds(pl.multiple_of(HALF + base + h, SUB), SUB)
                    mirror = pl.ds(pl.multiple_of(HALF - SUB - base - h, SUB), SUB)
                    fr_c, fr_s = field(ph[sl, straight], ap[sl, straight].astype(F32))
                    fl_c, fl_s = field(lane_rev(ph[sl, mirror]), lane_rev(ap[sl, mirror]).astype(F32))
                    ec, es = fr_c + fl_c, fr_s + fl_s
                    oc, os = fr_c - fl_c, fr_s - fl_s
                    for w in range(WL):
                        dc, ds = dx[w][0][:, here], dx[w][1][:, here]
                        e_s[w, 0, sl, there] = (ec * dc - es * ds).astype(BF16)
                        e_s[w, 1, sl, there] = (ec * ds + es * dc).astype(BF16)
                        o_s[w, 0, sl, there] = (oc * dc - os * ds).astype(BF16)
                        o_s[w, 1, sl, there] = (oc * ds + os * dc).astype(BF16)
            return 0

        lax.fori_loop(0, ROWS // STEP, rows, 0)

        return 0

    lax.fori_loop(0, blocks, block, 0)
    def dots(w, _):
        c = jnp.concatenate([tab[w, 0], ones], axis=0)
        s = tab[w, 1]
        for part in range(2):
            xacc[w, part] = nt(c, e_s[w, part])
            yacc[w, part] = nt(s, o_s[w, part])
        return 0

    lax.fori_loop(0, WL, dots, 0)
    j = flip_matrix(row < 8, ROWS)
    pos = row * ROWS + lax.broadcasted_iota(jnp.int32, (1, ROWS), 1)
    for w in range(WL):
        dc, ds = chirp_rows(level[w], pos)
        xr, xi = xacc[w, 0], xacc[w, 1]
        yr, yi = yacc[w, 0], yacc[w, 1]
        xr, xi = xr * dc - xi * ds, xr * ds + xi * dc
        yr, yi = yr * dc - yi * ds, yr * ds + yi * dc
        x0 = (xr[K : K + 1], xi[K : K + 1])
        xr, xi = xr[:K], xi[:K]
        plus = (xr + yi, xi - yr)
        minus = (xr - yi, xi + yr)
        for part in range(2):
            tmp[pl.ds(8, K), :] = plus[part]
            tmp[pl.ds(7, 1), :] = x0[part]
            p = nn(tmp[pl.ds(7, K), :].astype(BF16), j).astype(BF16)
            m = nn(minus[part].astype(BF16), j).astype(BF16)
            at = (w * 2 + part) * GRP
            for g in range(8):
                out[8 + g, at : at + GRP, :] = p[g * GRP : (g + 1) * GRP]
                out[7 - g, at : at + GRP, :] = m[g * GRP : (g + 1) * GRP]


def side_kernel(ph_r, ph_l, ap_r, ap_l, far, tab, tab2, fld):
    i = pl.program_id(0)
    write_tables(tab, i * CB, 0, 0)
    far[...] = tab[...]
    write_tables(tab2, i * CB, WL, 0)

    def rows(t, _):
        sl = pl.ds(pl.multiple_of(t * CHUNK, CHUNK), CHUNK)
        fld[0, sl, :], fld[1, sl, :] = field(ph_r[sl, :], ap_r[sl, :].astype(F32))
        fld[2, sl, :], fld[3, sl, :] = field(lane_rev(ph_l[sl, :]), lane_rev(ap_l[sl, :]).astype(F32))
        return 0

    lax.fori_loop(0, PART // CHUNK, rows, 0)


def focal_kernel(x, far, seen, out, obs, tab, sem):
    fetch = []
    for i in range(STEPS):
        cols = slice(i * BLK, (i + 1) * BLK)
        fetch.append(
            pltpu.make_async_copy(far.at[:WL, :, :, cols], tab.at[:, :, :, cols], sem.at[i])
        )
        fetch[-1].start()
    low = lax.axis_index("row") < 8
    for w in range(WL):
        for r in range(GRP):
            obs[w, pl.ds(jnp.where(low, GRP - 1 - r, r), 1), :] = seen[w, r : r + 1, :]
    last = lax.broadcasted_iota(jnp.int32, (GRP, K), 1) == K - 1
    acc = [[jnp.zeros((2 * GRP, K), F32)] * 2 + [jnp.zeros((2 * GRP, BLK), F32)] for w in range(WL)]
    for i in range(STEPS):
        fetch[i].wait()
        cols = slice(i * BLK, (i + 1) * BLK)
        for w in range(WL):
            at = w * 2 * GRP
            r = x[8 + i, at : at + 2 * GRP, :].astype(F32)
            l = x[7 - i, at : at + 2 * GRP, :].astype(F32)
            e = r + l
            acc[w][0] = acc[w][0] + nt(e.astype(BF16), tab[w, 0, :, cols])
            acc[w][1] = acc[w][1] + nt((r - l).astype(BF16), tab[w, 1, :, cols])
            acc[w][2] = acc[w][2] + e
    for w in range(WL):
        at = w * 2 * GRP
        acc_c, acc_s, centre = acc[w]
        centre = jnp.sum(centre, axis=1, keepdims=True) * NORM
        cr, ci = acc_c[:GRP], acc_c[GRP:]
        sr, si = acc_s[:GRP], acc_s[GRP:]
        rest = pltpu.roll(obs[w, :, K:], K - 1, 1)
        weighted = []
        for side, (fr, fi) in enumerate(
            (
                (jnp.where(last, centre[:GRP], cr + si), jnp.where(last, centre[GRP:], ci - sr)),
                (cr - si, ci + sr),
            )
        ):
            misfit = fr * fr + fi * fi - (rest if side == 0 else lane_rev(obs[w, :, :K]))
            weighted.append(
                [(misfit * fr).astype(BF16).astype(F32), (misfit * fi).astype(BF16).astype(F32)]
            )
        (pr, pi), (mr, mi) = weighted
        centre = jnp.concatenate([pr[:, K - 1 :], pi[:, K - 1 :]], axis=0) * NORM
        p = jnp.concatenate([jnp.where(last, 0.0, pr), jnp.where(last, 0.0, pi)], axis=0)
        m = jnp.concatenate([mr, mi], axis=0)
        s = (p + m).astype(BF16)
        d = (p - m).astype(BF16)
        for i in range(STEPS):
            cols = slice(i * BLK, (i + 1) * BLK)
            bc = nn(s, tab[w, 0, :, cols]) + centre
            bs = nn(d, tab[w, 1, :, cols])
            bcr, bci, bsr, bsi = bc[:GRP], bc[GRP:], bs[:GRP], bs[GRP:]
            for block, re, im in ((8 + i, bcr - bsi, bci + bsr), (7 - i, bcr + bsi, bci - bsr)):
                re, im = re.astype(BF16), im.astype(BF16)
                for q in range(PAIR):
                    p = q if block >= 8 else PAIR - 1 - q
                    lanes = slice(p * PART, (p + 1) * PART)
                    out[q * 16 + block, at : at + GRP, :] = re[:, lanes]
                    out[q * 16 + block, at + GRP : at + 2 * GRP, :] = im[:, lanes]


def gradient_kernel(level, x, tab, tab2, fld, out, lhs, mid, sp, tmp):
    row = lax.axis_index("row")
    lo = lax.axis_index("band_lo")
    flip = row < 8
    j = flip_matrix(flip, PART)
    lane = lax.broadcasted_iota(jnp.int32, (1, PART), 1)
    pos = row * ROWS + lo * PART + jnp.where(flip, PART - 1 - lane, lane)
    for w in range(PAIR * WL):
        src = (lo + w // WL) % PAIR * 16
        dc, ds = chirp_rows(level[w], pos)
        p, m, b0 = [], [], []
        for part in range(2):
            at = (w % WL * 2 + part) * GRP
            for g in range(8):
                tmp[g * GRP : (g + 1) * GRP, :] = x[src + 8 + g, at : at + GRP, :].astype(F32)
            tmp[K : K + 8, :] = jnp.zeros((8, PART), F32)
            b0.append(tmp[0:1, :])
            p.append(tmp[pl.ds(1, K), :])
            m.append(
                jnp.concatenate([x[src + 7 - g, at : at + GRP, :] for g in range(8)], axis=0).astype(F32)
            )
        for n, (re, im) in enumerate(
            ((p[0] + m[0], p[1] + m[1]), (p[0] - m[0], p[1] - m[1]))
        ):
            lhs[w, n, :PART] = nt(j, (re * dc + im * ds).astype(BF16)).astype(BF16)
            lhs[w, n, PART:] = nt(j, (im * dc - re * ds).astype(BF16)).astype(BF16)
        for part, v in enumerate((b0[0] * dc + b0[1] * ds, b0[1] * dc - b0[0] * ds)):
            v = jnp.broadcast_to((v * NORM).astype(BF16), (128, PART))
            mid[w, part] = nt(j, v)

    def block(i, _):
        base = pl.multiple_of(i * CB, CB)
        dx = [chirp_cols(level[w], base, CB) for w in range(PAIR * WL)]
        per = M // CB
        right = 4 + i // per, pl.multiple_of(i % per * CB, CB)
        left = 3 - i // per, pl.multiple_of((per - 1 - i % per) * CB, CB)
        for h in range(0, CB, SUB):
            cols = pl.ds(pl.multiple_of(base + h, SUB), SUB)
            for w in range(PAIR * WL):
                table = tab if w < WL else tab2
                for n in range(2):
                    sp[w, n, :, h : h + SUB] = nn(lhs[w, n], table[w % WL, n, :, cols])
            for r0 in range(0, PART, CHUNK):
                sl = slice(r0, r0 + CHUNK)
                im = slice(PART + r0, PART + r0 + CHUNK)
                tot = [0.0, 0.0, 0.0, 0.0]
                for w in range(PAIR * WL):
                    dc, ds = dx[w][0][:, h : h + SUB], dx[w][1][:, h : h + SUB]
                    m = [
                        jnp.concatenate([mid[w, part, sl, :]] * (SUB // 128), axis=1)
                        for part in range(2)
                    ]
                    cr, ci = sp[w, 0, sl, h : h + SUB] + m[0], sp[w, 0, im, h : h + SUB] + m[1]
                    sr, si = sp[w, 1, sl, h : h + SUB], sp[w, 1, im, h : h + SUB]
                    tot[0] += cr * dc + ci * ds
                    tot[1] += ci * dc - cr * ds
                    tot[2] += sr * dc + si * ds
                    tot[3] += si * dc - sr * ds
                cr, ci, sr, si = tot
                g_r = (ci + sr) * fld[0, sl, cols] - (cr - si) * fld[1, sl, cols]
                g_l = (ci - sr) * fld[2, sl, cols] - (cr + si) * fld[3, sl, cols]
                out[right[0], sl, pl.ds(right[1] + h, SUB)] = g_r.astype(BF16)
                out[left[0], sl, pl.ds(left[1] + (CB - SUB - h), SUB)] = lane_rev(g_l).astype(BF16)
        return 0

    lax.fori_loop(0, HALF // CB, block, 0)


def run_forward(level, phase, aperture):
    any_space = pl.BlockSpec(memory_space=pl.ANY)
    return pl.pallas_call(
        forward_kernel,
        out_shape=jax.ShapeDtypeStruct((16, WL * 2 * GRP, ROWS), BF16),
        in_specs=[pl.BlockSpec(memory_space=pltpu.SMEM), any_space, any_space],
        out_specs=pl.BlockSpec(memory_space=pltpu.VMEM),
        scratch_shapes=[pltpu.VMEM((WL, 2, ROWS, HALF), BF16)] * 2
        + [
            pltpu.VMEM((ROWS, N), F32),
            pltpu.VMEM((ROWS, N), jnp.int32),
            pltpu.VMEM((WL, 2, K, HALF), BF16),
            pltpu.VMEM((WL, 2, K + 16, ROWS), F32),
            pltpu.VMEM((WL, 2, K, ROWS), F32),
            pltpu.VMEM((K + 16, ROWS), F32),
            pltpu.SemaphoreType.DMA((HALF // CB, 4)),
        ],
        compiler_params=pltpu.CompilerParams(vmem_limit_bytes=FWD_VMEM * 2**20),
        name="forward",
    )(level, phase, aperture)


def run_side(phase, aperture):
    right = pl.BlockSpec((PART, CB), lambda i: (lax.axis_index("band_lo"), HALF // CB + i))
    left = pl.BlockSpec((PART, CB), lambda i: (lax.axis_index("band_lo"), HALF // CB - 1 - i))
    return pl.pallas_call(
        side_kernel,
        grid=(HALF // CB,),
        out_shape=(
            jax.ShapeDtypeStruct((FAR * WL, 2, K, HALF), BF16),
            jax.ShapeDtypeStruct((WL, 2, K, HALF), BF16),
            jax.ShapeDtypeStruct((WL, 2, K, HALF), BF16),
            jax.ShapeDtypeStruct((4, PART, HALF), F32),
        ),
        in_specs=[right, left, right, left],
        out_specs=(
            pl.BlockSpec((WL, 2, K, CB), lambda i: (0, 0, 0, i)),
            pl.BlockSpec((WL, 2, K, CB), lambda i: (0, 0, 0, i)),
            pl.BlockSpec((WL, 2, K, CB), lambda i: (0, 0, 0, i)),
            pl.BlockSpec((4, PART, CB), lambda i: (0, 0, i)),
        ),
        compiler_params=pltpu.CompilerParams(vmem_limit_bytes=SIDE_VMEM * 2**20),
        cost_estimate=pl.CostEstimate(flops=2**32, bytes_accessed=2**24, transcendentals=0),
        name="side",
    )(phase, phase, aperture, aperture)


def run_focal(x, tab, seen):
    return pl.pallas_call(
        focal_kernel,
        out_shape=jax.ShapeDtypeStruct((PAIR * 16, WL * 2 * GRP, PART), BF16),
        in_specs=[
            pl.BlockSpec(memory_space=pltpu.VMEM),
            pl.BlockSpec(memory_space=pl.ANY),
            pl.BlockSpec(memory_space=pltpu.VMEM),
        ],
        out_specs=pl.BlockSpec(memory_space=pltpu.VMEM),
        scratch_shapes=[
            pltpu.VMEM((WL, GRP, M), F32),
            pltpu.VMEM((WL, 2, K, HALF), BF16),
            pltpu.SemaphoreType.DMA((STEPS,)),
        ],
        compiler_params=pltpu.CompilerParams(vmem_limit_bytes=40 * 2**20),
        cost_estimate=pl.CostEstimate(flops=2**34, bytes_accessed=2**26, transcendentals=0),
        name="focal",
    )(x, tab, seen)


def run_gradient(level, x, tab, tab2, fld):
    return pl.pallas_call(
        gradient_kernel,
        out_shape=jax.ShapeDtypeStruct((8, PART, M), BF16),
        in_specs=[pl.BlockSpec(memory_space=pltpu.SMEM)] + [pl.BlockSpec(memory_space=pltpu.VMEM)] * 4,
        out_specs=pl.BlockSpec(memory_space=pltpu.VMEM),
        scratch_shapes=[
            pltpu.VMEM((PAIR * WL, 2, 2 * PART, K), BF16),
            pltpu.VMEM((PAIR * WL, 2, PART, 128), F32),
            pltpu.VMEM((PAIR * WL, 2, 2 * PART, CB), F32),
            pltpu.VMEM((K + 8, PART), F32),
        ],
        compiler_params=pltpu.CompilerParams(vmem_limit_bytes=28 * 2**20),
        cost_estimate=pl.CostEstimate(flops=2**34, bytes_accessed=2**26, transcendentals=0),
        name="gradient",
    )(level, x, tab, tab2, fld)


def local(phase, aperture, defocus_index, intensity):
    level = defocus_index.astype(jnp.int32)
    levels = jnp.concatenate([level, lax.ppermute(level, "band_lo", [(0, 1), (1, 0)])])
    sent = run_forward(level, phase, aperture)
    sent, levels, phase, aperture = lax.optimization_barrier((sent, levels, phase, aperture))
    got = lax.all_to_all(sent, "row", 0, 0, tiled=True)
    far, tab, tab2, fld = run_side(phase, aperture)
    got, far, tab, tab2, fld = lax.optimization_barrier((got, far, tab, tab2, fld))
    sent = run_focal(got, far, intensity)
    got = lax.all_to_all(sent, ("band_lo", "row"), 0, 0, tiled=True)
    parts = run_gradient(levels, got, tab, tab2, fld)
    parts = lax.all_to_all(parts, ("band_hi", "band_lo"), 0, 0, tiled=True)
    return jnp.sum(parts.reshape(8 // PAIR, ROWS, M).astype(F32), axis=0)


def solution(mesh):
    band, row = mesh.devices.shape
    split = Mesh(mesh.devices.reshape(band // PAIR, PAIR, row), ("band_hi", "band_lo", "row"))
    both = ("band_hi", "band_lo")
    return jax.shard_map(
        local,
        mesh=split,
        in_specs=(P("row", None), P("row", None), P(both), P(both, "row", None)),
        out_specs=P("row", both),
        check_vma=False,
    )
```

```python
import math

import jax
import jax.numpy as jnp
from jax import lax
from jax.experimental import pallas as pl
from jax.experimental.pallas import tpu as pltpu
from jax.sharding import Mesh
from jax.sharding import PartitionSpec as P

F32 = jnp.float32
BF16 = jnp.bfloat16
N = 4096
M = 512
HALF = N // 2
K = M // 2
ROWS = 256
BLK = 256
CB = 512
SUB = 256
FWD_VMEM = 57
SIDE_VMEM = 57
FAR = 8
WIDE = 512
STEP = 256
DOT = 512
CHUNK = 32
STEPS = HALF // BLK
WL = 2
GRP = 32
PAIR = 2
PART = ROWS // PAIR
NORM = 1.0 / math.sqrt(N)

SIN_C = (9.99999246e-01, -1.66656827e-01, 8.31325871e-03, -1.85243573e-04)
COS_C = (9.99999953e-01, -4.99999053e-01, 4.16635847e-02, -1.38537043e-03, 2.31539316e-05)
SIN_T = (6.28318492, -41.34159016, 81.5999729, -76.61480386, 41.34439753, -12.47366849)
COS_T = (0.99999999, -19.73920453, 64.93911898, -85.45016555, 60.16783172, -25.96831326, 6.52961036)


def poly(coefs, y):
    acc = coefs[-1]
    for c in coefs[-2::-1]:
        acc = acc * y + c
    return acc


def turn(t):
    t = t - jnp.floor(t + 0.5)
    y = t * t
    return poly(COS_T, y), t * poly(SIN_T, y)


def unit(phi):
    y = phi * phi
    r2 = math.sqrt(2.0)
    c = poly([r2 * v / 4.0**n for n, v in enumerate(COS_C)], y)
    s = phi * poly([0.5 * r2 * v / 4.0**n for n, v in enumerate(SIN_C)], y)
    return c, s


def field(phi, amp):
    c, s = unit(phi)
    a_s = amp * s
    return amp - s * a_s, a_s * c


def lane_rev(x):
    rows, lanes = x.shape
    idx = 127 - lax.broadcasted_iota(jnp.int32, (rows, 128), 1)
    parts = [
        jnp.take_along_axis(x[:, s : s + 128], idx, axis=1, mode="promise_in_bounds")
        for s in range(lanes - 128, -1, -128)
    ]
    return jnp.concatenate(parts, axis=1) if len(parts) > 1 else parts[0]


def nt(a, b):
    return lax.dot_general(a, b, (((1,), (1,)), ((), ())), preferred_element_type=F32)


def nn(a, b):
    return lax.dot_general(a, b, (((1,), (0,)), ((), ())), preferred_element_type=F32)


def span(w):
    lo = lax.axis_index("band_lo")
    wave = lax.axis_index("band_hi") * (PAIR * WL) + (lo * WL + w) % (PAIR * WL)
    return (1024 * (16 + wave)).astype(F32)


def angle(n, m):
    inv = 1.0 / m
    q = jnp.floor(n * inv + 0.5)
    return turn((n - q * m) * inv)


def chirp_cols(level, first, lanes):
    x = (2 * (first + lax.broadcasted_iota(jnp.int32, (1, lanes), 1)) + 1).astype(F32)
    return turn(x * x * (level.astype(F32) * (0.5 / (N * N))))


def chirp_rows(level, row_pos):
    x = (2 * row_pos - (N - 1)).astype(F32)
    return turn(x * x * (level.astype(F32) * (0.5 / (N * N))))


def flip_matrix(flip, size):
    r = lax.broadcasted_iota(jnp.int32, (size, size), 0)
    c = lax.broadcasted_iota(jnp.int32, (size, size), 1)
    return jnp.where(jnp.where(flip, size - 1 - c, c) == r, 1.0, 0.0).astype(BF16)


def write_tables(tab, first, wave0, place):
    k = lax.broadcasted_iota(jnp.int32, (8, 128), 0) + 1
    lane = lax.broadcasted_iota(jnp.int32, (8, 128), 1)
    at, state = [], []
    for w in range(WL):
        m = span(wave0 + w)
        for t in range(0, CB, 128):
            x = 2 * (first + t + lane) + 1
            c, s = angle((x * k).astype(F32), m)
            rc, rs = angle((x * 8).astype(F32), m)
            at.append((w, pl.ds(pl.multiple_of(place + t, 128), 128)))
            state.append((c * NORM, s * NORM, rc, rs))
    for q in range(K // 16):
        rows = slice(16 * q, 16 * q + 16)
        for n, (w, lanes) in enumerate(at):
            c0, s0, rc, rs = state[n]
            c1, s1 = c0 * rc - s0 * rs, c0 * rs + s0 * rc
            tab[w, 0, rows, lanes] = jnp.concatenate([c0, c1], axis=0).astype(BF16)
            tab[w, 1, rows, lanes] = jnp.concatenate([s0, s1], axis=0).astype(BF16)
            state[n] = (c1 * rc - s1 * rs, c1 * rs + s1 * rc, rc, rs)


def forward_kernel(level, ph_in, ap_in, out, *scratch):
    e_s, o_s, ph, ap, tab, xacc, yacc, tmp, sem_in = scratch
    row = lax.axis_index("row")
    blocks = HALF // CB

    def right(i):
        return pl.ds(pl.multiple_of(HALF + i * CB, CB), CB)

    def left(i):
        return pl.ds(pl.multiple_of(HALF - CB - i * CB, CB), CB)

    def fetch(i):
        return [
            pltpu.make_async_copy(src.at[:, cols], dst.at[:, cols], sem_in.at[i, n])
            for n, (src, dst, cols) in enumerate(
                ((ph_in, ph, right(i)), (ph_in, ph, left(i)), (ap_in, ap, right(i)), (ap_in, ap, left(i)))
            )
        ]

    for i in range(blocks):
        for copy in fetch(i):
            copy.start()
    ones = jnp.full((16, HALF), NORM, BF16)

    def block(i, _):
        base = pl.multiple_of(i * CB, CB)
        cols = pl.ds(base, CB)

        def tables(n, _):
            write_tables(tab, base, 0, base)
            return 0

        lax.fori_loop(0, jnp.minimum(i + 1, 1), tables, 0)
        for copy in fetch(i):
            copy.wait()
        dx = [chirp_cols(level[w], base, CB) for w in range(WL)]

        def rows(t, _):
            for r1 in range(0, STEP, CHUNK):
                for h in range(0, CB, SUB):
                    sl = pl.ds(pl.multiple_of(t * STEP + r1, CHUNK), CHUNK)
                    here = slice(h, h + SUB)
                    there = pl.ds(pl.multiple_of(base + h, SUB), SUB)
                    straight = pl.ds(pl.multiple_of(HALF + base + h, SUB), SUB)
                    mirror = pl.ds(pl.multiple_of(HALF - SUB - base - h, SUB), SUB)
                    fr_c, fr_s = field(ph[sl, straight], ap[sl, straight].astype(F32))
                    fl_c, fl_s = field(lane_rev(ph[sl, mirror]), lane_rev(ap[sl, mirror]).astype(F32))
                    ec, es = fr_c + fl_c, fr_s + fl_s
                    oc, os = fr_c - fl_c, fr_s - fl_s
                    for w in range(WL):
                        dc, ds = dx[w][0][:, here], dx[w][1][:, here]
                        e_s[w, 0, sl, there] = (ec * dc - es * ds).astype(BF16)
                        e_s[w, 1, sl, there] = (ec * ds + es * dc).astype(BF16)
                        o_s[w, 0, sl, there] = (oc * dc - os * ds).astype(BF16)
                        o_s[w, 1, sl, there] = (oc * ds + os * dc).astype(BF16)
            return 0

        lax.fori_loop(0, ROWS // STEP, rows, 0)

        return 0

    lax.fori_loop(0, blocks, block, 0)
    def dots(w, _):
        c = jnp.concatenate([tab[w, 0], ones], axis=0)
        s = tab[w, 1]
        for part in range(2):
            xacc[w, part] = nt(c, e_s[w, part])
            yacc[w, part] = nt(s, o_s[w, part])
        return 0

    lax.fori_loop(0, WL, dots, 0)
    j = flip_matrix(row < 8, ROWS)
    pos = row * ROWS + lax.broadcasted_iota(jnp.int32, (1, ROWS), 1)
    for w in range(WL):
        dc, ds = chirp_rows(level[w], pos)
        xr, xi = xacc[w, 0], xacc[w, 1]
        yr, yi = yacc[w, 0], yacc[w, 1]
        xr, xi = xr * dc - xi * ds, xr * ds + xi * dc
        yr, yi = yr * dc - yi * ds, yr * ds + yi * dc
        x0 = (xr[K : K + 1], xi[K : K + 1])
        xr, xi = xr[:K], xi[:K]
        plus = (xr + yi, xi - yr)
        minus = (xr - yi, xi + yr)
        for part in range(2):
            tmp[pl.ds(8, K), :] = plus[part]
            tmp[pl.ds(7, 1), :] = x0[part]
            p = nn(tmp[pl.ds(7, K), :].astype(BF16), j).astype(BF16)
            m = nn(minus[part].astype(BF16), j).astype(BF16)
            at = (w * 2 + part) * GRP
            for g in range(8):
                out[8 + g, at : at + GRP, :] = p[g * GRP : (g + 1) * GRP]
                out[7 - g, at : at + GRP, :] = m[g * GRP : (g + 1) * GRP]


def side_kernel(ph_r, ph_l, ap_r, ap_l, far, tab, tab2, fld):
    i = pl.program_id(0)
    write_tables(tab, i * CB, 0, 0)
    far[...] = tab[...]
    write_tables(tab2, i * CB, WL, 0)

    def rows(t, _):
        sl = pl.ds(pl.multiple_of(t * CHUNK, CHUNK), CHUNK)
        fld[0, sl, :], fld[1, sl, :] = field(ph_r[sl, :], ap_r[sl, :].astype(F32))
        fld[2, sl, :], fld[3, sl, :] = field(lane_rev(ph_l[sl, :]), lane_rev(ap_l[sl, :]).astype(F32))
        return 0

    lax.fori_loop(0, PART // CHUNK, rows, 0)


def focal_kernel(x, far, seen, out, obs, tab, sem):
    fetch = []
    for i in range(STEPS):
        cols = slice(i * BLK, (i + 1) * BLK)
        fetch.append(
            pltpu.make_async_copy(far.at[:WL, :, :, cols], tab.at[:, :, :, cols], sem.at[i])
        )
        fetch[-1].start()
    low = lax.axis_index("row") < 8
    for w in range(WL):
        for r in range(GRP):
            obs[w, pl.ds(jnp.where(low, GRP - 1 - r, r), 1), :] = seen[w, r : r + 1, :]
    last = lax.broadcasted_iota(jnp.int32, (GRP, K), 1) == K - 1
    acc = [[jnp.zeros((2 * GRP, K), F32)] * 2 + [jnp.zeros((2 * GRP, BLK), F32)] for w in range(WL)]
    for i in range(STEPS):
        fetch[i].wait()
        cols = slice(i * BLK, (i + 1) * BLK)
        for w in range(WL):
            at = w * 2 * GRP
            r = x[8 + i, at : at + 2 * GRP, :].astype(F32)
            l = x[7 - i, at : at + 2 * GRP, :].astype(F32)
            e = r + l
            acc[w][0] = acc[w][0] + nt(e.astype(BF16), tab[w, 0, :, cols])
            acc[w][1] = acc[w][1] + nt((r - l).astype(BF16), tab[w, 1, :, cols])
            acc[w][2] = acc[w][2] + e
    for w in range(WL):
        at = w * 2 * GRP
        acc_c, acc_s, centre = acc[w]
        centre = jnp.sum(centre, axis=1, keepdims=True) * NORM
        cr, ci = acc_c[:GRP], acc_c[GRP:]
        sr, si = acc_s[:GRP], acc_s[GRP:]
        rest = pltpu.roll(obs[w, :, K:], K - 1, 1)
        weighted = []
        for side, (fr, fi) in enumerate(
            (
                (jnp.where(last, centre[:GRP], cr + si), jnp.where(last, centre[GRP:], ci - sr)),
                (cr - si, ci + sr),
            )
        ):
            misfit = fr * fr + fi * fi - (rest if side == 0 else lane_rev(obs[w, :, :K]))
            weighted.append(
                [(misfit * fr).astype(BF16).astype(F32), (misfit * fi).astype(BF16).astype(F32)]
            )
        (pr, pi), (mr, mi) = weighted
        centre = jnp.concatenate([pr[:, K - 1 :], pi[:, K - 1 :]], axis=0) * NORM
        p = jnp.concatenate([jnp.where(last, 0.0, pr), jnp.where(last, 0.0, pi)], axis=0)
        m = jnp.concatenate([mr, mi], axis=0)
        s = (p + m).astype(BF16)
        d = (p - m).astype(BF16)
        for i in range(STEPS):
            cols = slice(i * BLK, (i + 1) * BLK)
            bc = nn(s, tab[w, 0, :, cols]) + centre
            bs = nn(d, tab[w, 1, :, cols])
            bcr, bci, bsr, bsi = bc[:GRP], bc[GRP:], bs[:GRP], bs[GRP:]
            for block, re, im in ((8 + i, bcr - bsi, bci + bsr), (7 - i, bcr + bsi, bci - bsr)):
                re, im = re.astype(BF16), im.astype(BF16)
                for q in range(PAIR):
                    p = q if block >= 8 else PAIR - 1 - q
                    lanes = slice(p * PART, (p + 1) * PART)
                    out[q * 16 + block, at : at + GRP, :] = re[:, lanes]
                    out[q * 16 + block, at + GRP : at + 2 * GRP, :] = im[:, lanes]


def gradient_kernel(level, x, tab, tab2, fld, out, lhs, mid, sp, tmp):
    row = lax.axis_index("row")
    lo = lax.axis_index("band_lo")
    flip = row < 8
    j = flip_matrix(flip, PART)
    lane = lax.broadcasted_iota(jnp.int32, (1, PART), 1)
    pos = row * ROWS + lo * PART + jnp.where(flip, PART - 1 - lane, lane)
    for w in range(PAIR * WL):
        src = (lo + w // WL) % PAIR * 16
        dc, ds = chirp_rows(level[w], pos)
        p, m, b0 = [], [], []
        for part in range(2):
            at = (w % WL * 2 + part) * GRP
            for g in range(8):
                tmp[g * GRP : (g + 1) * GRP, :] = x[src + 8 + g, at : at + GRP, :].astype(F32)
            tmp[K : K + 8, :] = jnp.zeros((8, PART), F32)
            b0.append(tmp[0:1, :])
            p.append(tmp[pl.ds(1, K), :])
            m.append(
                jnp.concatenate([x[src + 7 - g, at : at + GRP, :] for g in range(8)], axis=0).astype(F32)
            )
        for n, (re, im) in enumerate(
            ((p[0] + m[0], p[1] + m[1]), (p[0] - m[0], p[1] - m[1]))
        ):
            lhs[w, n, :PART] = nt(j, (re * dc + im * ds).astype(BF16)).astype(BF16)
            lhs[w, n, PART:] = nt(j, (im * dc - re * ds).astype(BF16)).astype(BF16)
        for part, v in enumerate((b0[0] * dc + b0[1] * ds, b0[1] * dc - b0[0] * ds)):
            v = jnp.broadcast_to((v * NORM).astype(BF16), (128, PART))
            mid[w, part] = nt(j, v)

    def block(i, _):
        base = pl.multiple_of(i * CB, CB)
        dx = [chirp_cols(level[w], base, CB) for w in range(PAIR * WL)]
        per = M // CB
        right = 4 + i // per, pl.multiple_of(i % per * CB, CB)
        left = 3 - i // per, pl.multiple_of((per - 1 - i % per) * CB, CB)
        for h in range(0, CB, WIDE):
            cols = pl.ds(pl.multiple_of(base + h, WIDE), WIDE)
            for w in range(PAIR * WL):
                table = tab if w < WL else tab2
                for n in range(2):
                    sp[w, n, :, h : h + WIDE] = nn(lhs[w, n], table[w % WL, n, :, cols])
            for r0 in range(0, PART, CHUNK):
                sl = slice(r0, r0 + CHUNK)
                im = slice(PART + r0, PART + r0 + CHUNK)
                tot = [0.0, 0.0, 0.0, 0.0]
                for w in range(PAIR * WL):
                    dc, ds = dx[w][0][:, h : h + WIDE], dx[w][1][:, h : h + WIDE]
                    m = [
                        jnp.concatenate([mid[w, part, sl, :]] * (WIDE // 128), axis=1)
                        for part in range(2)
                    ]
                    cr, ci = sp[w, 0, sl, h : h + WIDE] + m[0], sp[w, 0, im, h : h + WIDE] + m[1]
                    sr, si = sp[w, 1, sl, h : h + WIDE], sp[w, 1, im, h : h + WIDE]
                    tot[0] += cr * dc + ci * ds
                    tot[1] += ci * dc - cr * ds
                    tot[2] += sr * dc + si * ds
                    tot[3] += si * dc - sr * ds
                cr, ci, sr, si = tot
                g_r = (ci + sr) * fld[0, sl, cols] - (cr - si) * fld[1, sl, cols]
                g_l = (ci - sr) * fld[2, sl, cols] - (cr + si) * fld[3, sl, cols]
                out[right[0], sl, pl.ds(right[1] + h, WIDE)] = g_r.astype(BF16)
                out[left[0], sl, pl.ds(left[1] + (CB - WIDE - h), WIDE)] = lane_rev(g_l).astype(BF16)
        return 0

    lax.fori_loop(0, HALF // CB, block, 0)


def run_forward(level, phase, aperture):
    any_space = pl.BlockSpec(memory_space=pl.ANY)
    return pl.pallas_call(
        forward_kernel,
        out_shape=jax.ShapeDtypeStruct((16, WL * 2 * GRP, ROWS), BF16),
        in_specs=[pl.BlockSpec(memory_space=pltpu.SMEM), any_space, any_space],
        out_specs=pl.BlockSpec(memory_space=pltpu.VMEM),
        scratch_shapes=[pltpu.VMEM((WL, 2, ROWS, HALF), BF16)] * 2
        + [
            pltpu.VMEM((ROWS, N), F32),
            pltpu.VMEM((ROWS, N), jnp.int32),
            pltpu.VMEM((WL, 2, K, HALF), BF16),
            pltpu.VMEM((WL, 2, K + 16, ROWS), F32),
            pltpu.VMEM((WL, 2, K, ROWS), F32),
            pltpu.VMEM((K + 16, ROWS), F32),
            pltpu.SemaphoreType.DMA((HALF // CB, 4)),
        ],
        compiler_params=pltpu.CompilerParams(vmem_limit_bytes=FWD_VMEM * 2**20),
        name="forward",
    )(level, phase, aperture)


def run_side(phase, aperture):
    right = pl.BlockSpec((PART, CB), lambda i: (lax.axis_index("band_lo"), HALF // CB + i))
    left = pl.BlockSpec((PART, CB), lambda i: (lax.axis_index("band_lo"), HALF // CB - 1 - i))
    return pl.pallas_call(
        side_kernel,
        grid=(HALF // CB,),
        out_shape=(
            jax.ShapeDtypeStruct((FAR * WL, 2, K, HALF), BF16),
            jax.ShapeDtypeStruct((WL, 2, K, HALF), BF16),
            jax.ShapeDtypeStruct((WL, 2, K, HALF), BF16),
            jax.ShapeDtypeStruct((4, PART, HALF), F32),
        ),
        in_specs=[right, left, right, left],
        out_specs=(
            pl.BlockSpec((WL, 2, K, CB), lambda i: (0, 0, 0, i)),
            pl.BlockSpec((WL, 2, K, CB), lambda i: (0, 0, 0, i)),
            pl.BlockSpec((WL, 2, K, CB), lambda i: (0, 0, 0, i)),
            pl.BlockSpec((4, PART, CB), lambda i: (0, 0, i)),
        ),
        compiler_params=pltpu.CompilerParams(vmem_limit_bytes=SIDE_VMEM * 2**20),
        cost_estimate=pl.CostEstimate(flops=2**32, bytes_accessed=2**24, transcendentals=0),
        name="side",
    )(phase, phase, aperture, aperture)


def run_focal(x, tab, seen):
    return pl.pallas_call(
        focal_kernel,
        out_shape=jax.ShapeDtypeStruct((PAIR * 16, WL * 2 * GRP, PART), BF16),
        in_specs=[
            pl.BlockSpec(memory_space=pltpu.VMEM),
            pl.BlockSpec(memory_space=pl.ANY),
            pl.BlockSpec(memory_space=pltpu.VMEM),
        ],
        out_specs=pl.BlockSpec(memory_space=pltpu.VMEM),
        scratch_shapes=[
            pltpu.VMEM((WL, GRP, M), F32),
            pltpu.VMEM((WL, 2, K, HALF), BF16),
            pltpu.SemaphoreType.DMA((STEPS,)),
        ],
        compiler_params=pltpu.CompilerParams(vmem_limit_bytes=40 * 2**20),
        cost_estimate=pl.CostEstimate(flops=2**34, bytes_accessed=2**26, transcendentals=0),
        name="focal",
    )(x, tab, seen)


def run_gradient(level, x, tab, tab2, fld):
    return pl.pallas_call(
        gradient_kernel,
        out_shape=jax.ShapeDtypeStruct((8, PART, M), BF16),
        in_specs=[pl.BlockSpec(memory_space=pltpu.SMEM)] + [pl.BlockSpec(memory_space=pltpu.VMEM)] * 4,
        out_specs=pl.BlockSpec(memory_space=pltpu.VMEM),
        scratch_shapes=[
            pltpu.VMEM((PAIR * WL, 2, 2 * PART, K), BF16),
            pltpu.VMEM((PAIR * WL, 2, PART, 128), F32),
            pltpu.VMEM((PAIR * WL, 2, 2 * PART, CB), F32),
            pltpu.VMEM((K + 8, PART), F32),
        ],
        compiler_params=pltpu.CompilerParams(vmem_limit_bytes=28 * 2**20),
        cost_estimate=pl.CostEstimate(flops=2**34, bytes_accessed=2**26, transcendentals=0),
        name="gradient",
    )(level, x, tab, tab2, fld)


def local(phase, aperture, defocus_index, intensity):
    level = defocus_index.astype(jnp.int32)
    levels = jnp.concatenate([level, lax.ppermute(level, "band_lo", [(0, 1), (1, 0)])])
    sent = run_forward(level, phase, aperture)
    sent, levels, phase, aperture = lax.optimization_barrier((sent, levels, phase, aperture))
    got = lax.all_to_all(sent, "row", 0, 0, tiled=True)
    far, tab, tab2, fld = run_side(phase, aperture)
    got, far, tab, tab2, fld = lax.optimization_barrier((got, far, tab, tab2, fld))
    sent = run_focal(got, far, intensity)
    got = lax.all_to_all(sent, ("band_lo", "row"), 0, 0, tiled=True)
    parts = run_gradient(levels, got, tab, tab2, fld)
    parts = lax.all_to_all(parts, ("band_hi", "band_lo"), 0, 0, tiled=True)
    return jnp.sum(parts.reshape(8 // PAIR, ROWS, M).astype(F32), axis=0)


def solution(mesh):
    band, row = mesh.devices.shape
    split = Mesh(mesh.devices.reshape(band // PAIR, PAIR, row), ("band_hi", "band_lo", "row"))
    both = ("band_hi", "band_lo")
    return jax.shard_map(
        local,
        mesh=split,
        in_specs=(P("row", None), P("row", None), P(both), P(both, "row", None)),
        out_specs=P("row", both),
        check_vma=False,
    )
```
